256 devices in a mesh: ta: 8 (over x, y_lo), af: 32 (over y_hi, z, core).
Axes of the slice: x: 4, y: 4 (y_hi: 2, y_lo: 2; y = y_hi * 2 + y_lo), z: 8, core: 2. Of those that a mesh axis runs over, the one named last changes fastest.
Arguments:
- activations: bfloat16 [32768, 4096], P(('ta', 'af')), may hold values from -24 to 24
- cotangent: bfloat16 [32768, 4096], P(('ta', 'af')), may hold values from -6 to 6
- masked: int32 [32768], P(('ta', 'af')), may hold values 0 or 1
- ratios: int32 [256], P(('ta', 'af')), may hold values from 100 to 1000
- owners: int32 [32], replicated, may hold values from 0 to 31, as said below
Outputs:
- update: float32 [4096, 4096], P('af')
The draws below stay inside these ranges and needn't reach their ends.
Inputs may be any that keep to these rules, and one draw needn't show every extreme that they name: `owners`: heads with the same value are orthogonalized together; no value is named by more than 2 heads, and one value by exactly 2.
All inputs are finite; a program needn't handle non-finite values. No bound on the sum of `masked` on one device may be relied on, other than what follows from the above.
Results may differ from the reference program's by a relative error of at most 0.03.
Values may be sent and summed in bfloat16 or wider, within the bound.
No kernel may reach another device: no remote copies, remote signals or barrier semaphores. Data moves between devices by JAX's collectives and lax.ppermute only.
A program may use at most 192 MiB of HBM per device.

```python
import math
import jax
import jax.numpy as jnp
from jax import lax

D = 4096
HD = 128
HEADS = 32
TOK_DEV = 128
NS_ITERS = 5
OWN_MAX = 2
SAMPLES = 256
TOKENS = 32768
N_AF = 32


def draw_owners(key, part):
    key = jax.random.fold_in(key, 7)
    key_first, key_slots, key_order = jax.random.split(key, 3)
    first_owner = jax.random.randint(key_first, (), 0, N_AF)
    slot_index = jnp.arange(N_AF * OWN_MAX - OWN_MAX)
    slot_list = jnp.where(slot_index < first_owner * OWN_MAX, slot_index, slot_index + OWN_MAX)
    slot_list = jax.random.permutation(key_slots, slot_list)
    others = slot_list[:HEADS - OWN_MAX] // OWN_MAX
    owners = jnp.concatenate([jnp.full((OWN_MAX,), first_owner), others]).astype(jnp.int32)
    return jax.random.permutation(key_order, owners)


def with_ends(values, key, least, largest):
    longest = values.shape.index(max(values.shape))
    spots = []
    for shift in (0, 1):
        where = [jax.random.randint(jax.random.fold_in(key, axis), (), 0, length) for axis, length in enumerate(values.shape)]
        where[longest] = (where[longest] + shift) % values.shape[longest]
        spots.append(tuple(where))
    return values.at[spots[0]].set(least).at[spots[1]].set(largest)


def strengthened(array, stream_key, source, target, blocks, factor):
    owner, partner = [(jnp.arange(array.shape[axis_at]) // (array.shape[axis_at] // blocks)).reshape([-1 if axis == axis_at else 1 for axis in range(array.ndim)]) for axis_at in (source, target)]
    chosen = jax.random.permutation(stream_key, blocks)[partner]
    strong = (owner == chosen) | (owner == (partner + blocks // 2) % blocks)
    return jnp.where(strong, factor * array, array)


def block_scale(own_key, extent, shards, low, top_value):
    factor_of, own = 1.0, jax.random.fold_in(own_key, 6)
    for position, parts in shards:
        draws = jnp.exp(jax.random.uniform(jax.random.fold_in(own, position), (parts,), jnp.float32, low / len(shards), top_value / len(shards)))
        factor_of = factor_of * jnp.repeat(draws, extent[position] // parts).reshape([-1 if axis == position else 1 for axis in range(len(extent))])
    return factor_of


def scatter_about(key, extent, width, limit, cuts=(), kind=jnp.bfloat16):
    gain = block_scale(key, extent, cuts, -0.22, 0.18) if cuts else 1.0
    drawn = jax.random.normal(key, extent, jnp.float32) * width * gain
    return jnp.minimum(jnp.maximum(drawn, -limit), limit).astype(kind)


def gaussian_with(rng, dims, deviation, limit, cuts, heavy, dtype=jnp.bfloat16):
    values = deviation * jax.random.normal(rng, dims, jnp.float32)
    if cuts:
        values = values * block_scale(rng, dims, cuts, -0.22, 0.18)
    return jnp.clip(strengthened(values, jax.random.fold_in(rng, 3), *heavy), -limit, limit).astype(dtype)


def setup_inputs(seed: int = 0) -> dict:
    streams_of = jax.random.split(jax.random.key(seed), 6)
    activations = gaussian_with(streams_of[0], (TOKENS, D), 1.0, 24.0, ((0, 256),), (0, 1, 256, 6.0))
    cotangent = scatter_about(streams_of[1], (TOKENS, HEADS * HD), 1.0, 6.0, ((0, 256),))
    masked = with_ends((jax.random.randint(streams_of[2], (TOKENS,), 0, 2) < 1).astype(jnp.int32), jax.random.fold_in(streams_of[2], 1), 0, 1)
    ratios = with_ends(jax.random.randint(streams_of[3], (SAMPLES,), 100, 1001), jax.random.fold_in(streams_of[3], 1), 100, 1000).astype(jnp.int32)
    owners = draw_owners(jax.random.fold_in(streams_of[5], 71), 0)
    return {"activations": activations, "cotangent": cotangent, "masked": masked, "ratios": ratios, "owners": owners}


quintic_a = 3.4445
quintic_b = -4.775
quintic_c = 2.0315
epsilon = 1e-07
highest = lax.Precision.HIGHEST

def owner_selection(owners, owner_count, head_count, slot_count):
    head_order = jnp.arange(head_count)
    same_owner = owners[:, None] == owners[None, :]
    earlier = head_order[None, :] < head_order[:, None]
    slot_rank = lax.optimization_barrier(jnp.sum(jnp.logical_and(same_owner, earlier), axis=1))
    groups = jnp.arange(owner_count)[:, None, None]
    slot_ids = jnp.arange(slot_count)[None, :, None]
    return jnp.logical_and(owners[None, None, :] == groups, slot_rank[None, None, :] == slot_ids)

def newton_local(matrix):
    frob_norm = jnp.sqrt(jnp.sum(matrix * matrix)) + epsilon
    iterate = matrix / frob_norm
    for turn in range(NS_ITERS):
        gram_now = jnp.einsum('ri,rj->ij', iterate, iterate, precision=highest)
        polynomial = quintic_b * gram_now + quintic_c * jnp.dot(gram_now, gram_now, precision=highest)
        iterate = quintic_a * iterate + jnp.dot(iterate, polynomial, precision=highest)
    return iterate

def reference(activations, cotangent, masked, ratios, owners):
    columns = HEADS * HD
    weight = masked.astype(jnp.float32) * 1000.0 / jnp.repeat(ratios, TOK_DEV).astype(jnp.float32)
    scaled = (cotangent.astype(jnp.float32) * weight[:, None]).astype(jnp.bfloat16)
    sample_x = activations.reshape(SAMPLES, TOK_DEV, D)
    sample_g = scaled.reshape(SAMPLES, TOK_DEV, columns)

    def accumulate(running, sample_pair):
        product = lax.dot_general(sample_pair[0], sample_pair[1], (((0,), (0,)), ((), ())), preferred_element_type=jnp.float32)
        return (running + lax.optimization_barrier(product.astype(jnp.bfloat16)).astype(jnp.float32), None)
    gradient, unused = lax.scan(accumulate, jnp.zeros((D, columns), jnp.float32), (sample_x, sample_g))
    head_grad = lax.optimization_barrier(gradient.astype(jnp.bfloat16)).astype(jnp.float32).reshape(D, HEADS, HD)
    selection = owner_selection(owners, N_AF, HEADS, OWN_MAX).astype(jnp.float32)

    def per_group(group_select):
        group_block = jnp.einsum('kh,rhd->rkd', group_select, head_grad, precision=highest).reshape(D, OWN_MAX * HD)
        return newton_local(group_block).reshape(D, OWN_MAX, HD)
    results = lax.map(per_group, selection)
    update = jnp.einsum('okh,orkd->rhd', selection, results, precision=highest) * math.sqrt(D)
    return update.reshape(D, columns)
```

```python
import jax
import jax.numpy as jnp
from jax import lax
from jax.experimental import pallas as pl
from jax.experimental.pallas import tpu as pltpu
from jax.sharding import Mesh
from jax.sharding import PartitionSpec as P

HEADS = 32
NS_ITERS = 5
quintic_a = 3.4445
quintic_b = -4.775
quintic_c = 2.0315
epsilon = 1e-07
highest = lax.Precision.HIGHEST

Y_AT, X_AT, ZH_AT, Z0_AT, CORE_AT, PAIRS_AT, PERM_AT = 0, 1, 2, 3, 4, 5, 8

HEAD = 128
SLOT = 2 * HEAD
BLOCK = 1024
HALF = 64

f32, bf16 = jnp.float32, jnp.bfloat16


def smem():
    return pl.BlockSpec(memory_space=pltpu.SMEM)


def vmem():
    return pl.BlockSpec(memory_space=pltpu.VMEM)


def local_kernel(body, outs, operands, mib, flops, name):
    moved = sum(o.size * o.dtype.itemsize for o in list(outs) + list(operands))
    return pl.pallas_call(
        body,
        out_shape=outs,
        in_specs=[smem()] + [vmem()] * (len(operands) - 1),
        out_specs=[vmem()] * len(outs),
        compiler_params=pltpu.CompilerParams(vmem_limit_bytes=mib * 2**20),
        cost_estimate=pl.CostEstimate(flops=flops, bytes_accessed=moved, transcendentals=0),
        name=name,
    )(*operands)


def shape(dims, dtype):
    return jax.ShapeDtypeStruct(dims, dtype)


def scalars(owners):
    order = jnp.arange(HEADS)
    same = owners[:, None] == owners[None, :]
    paired = jnp.sum(same, axis=1) > 1
    first = jnp.min(jnp.where(same, order[None, :], HEADS), axis=1)
    key = jnp.where(paired, 0, HEADS * HEADS) + first * HEADS + order
    place = jnp.sum(key[None, :] < key[:, None], axis=1)
    perm = jnp.sum(jnp.where(place[:, None] == order[None, :], order[:, None], 0), axis=0)
    pairs = jnp.sum(paired) // 2
    here = [
        lax.axis_index("yhi") * 2 + lax.axis_index("ylo"),
        lax.axis_index("x"),
        lax.axis_index("zh"),
        lax.axis_index("z0"),
        lax.axis_index("core"),
        pairs,
        pairs,
        pairs,
    ]
    return jnp.concatenate([jnp.stack([v.astype(jnp.int32) for v in here]), perm.astype(jnp.int32)])


def prepare(meta, act, cot, weight, *outs):
    rows_out, cols_out = outs[:4], outs[4:]
    width = act.shape[1]
    for k in range(4):
        y = (meta[Y_AT] + k) & 3
        base = (y >> 1) * (width // 2)
        low = (y & 1) * HALF
        for crel in range(2):
            for zrel in range(2):
                for zh in range(4):
                    block = zh * 4 + (meta[Z0_AT] ^ zrel) * 2 + (meta[CORE_AT] ^ crel)
                    at = pl.multiple_of(base + block * 128, 128)
                    turned = act[:, pl.ds(at, 128)].T
                    part = jnp.where(low == 0, turned[:HALF], turned[HALF:])
                    to = ((crel * 2 + zrel) * 4 + zh) * HALF
                    rows_out[k][to : to + HALF, :] = part
    w = weight[...]
    for k in range(4):
        x = (meta[X_AT] + k) & 3
        for j in range(8):
            slot = x * 4 + ((meta[ZH_AT] + j // 2) & 3)
            head = meta[PERM_AT + slot * 2 + j % 2]
            at = pl.multiple_of(head * HEAD, HEAD)
            cols_out[k][:, j * HEAD : (j + 1) * HEAD] = (cot[:, pl.ds(at, HEAD)].astype(f32) * w).astype(
                bf16
            )


def multiply(meta, r0, r1, r3, r2a, r2b, g0, g1, g3, g2a, g2b, keep, send):
    tok = r0.shape[2]

    def rows_of(dx, dy):
        if dx == 2:
            return (r2a if dy < 2 else r2b)[dy % 2]
        return {0: r0, 1: r1, 3: r3}[dx][dy]

    def cols_of(dx, dy, at):
        ref = (g2a if dx < 2 else g2b) if dy == 2 else {0: g0, 1: g1, 3: g3}[dy]
        return ref[dx % 2 if dy == 2 else dx, :, pl.ds(at, SLOT)]

    for n in range(BLOCK // SLOT):
        total = jnp.zeros((BLOCK, SLOT), f32)
        for dx in range(4):
            left = jnp.concatenate([rows_of(dx, dy) for dy in range(4)], axis=1)
            right = jnp.concatenate([cols_of(dx, dy, n * SLOT) for dy in range(4)], axis=0)
            total = total + jnp.dot(left, right, preferred_element_type=f32)
        total = total.astype(bf16)
        for zrel in range(2):
            keep[zrel * 4 + n] = total[zrel * 256 : (zrel + 1) * 256]
            send[zrel * 4 + n] = total[512 + zrel * 256 : 512 + (zrel + 1) * 256]


def add_cores(meta, mine, other, *outs):
    for i, out in enumerate(outs):
        out[...] = (mine[i].astype(f32) + other[i].astype(f32)).astype(bf16)


def gram_part(meta, *refs):
    terms, (head_grad, keep, send, whole) = refs[:8], refs[8:]
    total = terms[0][...].astype(f32)
    for term in terms[1:]:
        total = total + term[...].astype(f32)
    part = total.astype(bf16)
    head_grad[...] = part
    whole[...] = lax.dot_general(part, part, (((0,), (0,)), ((), ())), preferred_element_type=f32)
    core = meta[CORE_AT]
    keep[...] = whole[pl.ds(pl.multiple_of(core * HEAD, HEAD), HEAD), :]
    send[...] = whole[pl.ds(pl.multiple_of((1 - core) * HEAD, HEAD), HEAD), :]


def newton(meta, mine, other, head_grad, o0, o1, o2, o3, result):
    core = meta[CORE_AT]
    a, b = mine[...], other[...]
    gram = jnp.concatenate([jnp.where(core == 0, a, b), jnp.where(core == 0, b, a)], axis=0)
    slot = meta[X_AT] * 4 + meta[ZH_AT]
    pair = slot < meta[PAIRS_AT]
    row = lax.broadcasted_iota(jnp.int32, (SLOT, SLOT), 0)
    col = lax.broadcasted_iota(jnp.int32, (SLOT, SLOT), 1)
    together = jnp.logical_or((row < HEAD) == (col < HEAD), pair)
    gram = jnp.where(together, gram, 0.0)
    on_diagonal = jnp.where(row == col, gram, 0.0)
    down = jnp.sum(on_diagonal, axis=0, keepdims=True)
    across = jnp.sum(on_diagonal, axis=1, keepdims=True)
    lane, line = col[:1, :], row[:, :1]

    def factor(squares, at, axis):
        low = jnp.sum(jnp.where(at < HEAD, squares, 0.0), axis=axis, keepdims=True)
        high = jnp.sum(jnp.where(at < HEAD, 0.0, squares), axis=axis, keepdims=True)
        norm = jnp.where(pair, low + high, jnp.where(at < HEAD, low, high))
        return 1.0 / (jnp.sqrt(norm) + epsilon)

    by_col = factor(down, lane, 1)
    by_row = factor(across, line, 0)
    gram = gram * by_row * by_col
    unit = jnp.where(row == col, 1.0, 0.0)
    dot = lambda p, q: jnp.dot(p, q, precision=highest, preferred_element_type=f32)
    product = None
    for turn in range(NS_ITERS):
        step = quintic_a * unit + quintic_b * gram + quintic_c * dot(gram, gram)
        if turn < NS_ITERS - 1:
            gram = dot(dot(gram, step), step)
        product = step if product is None else dot(product, step)
    top = product.astype(bf16)
    rest = product - top.astype(f32)
    middle = rest.astype(bf16)
    bottom = (rest - middle.astype(f32)).astype(bf16)
    h = head_grad[...]
    update = jnp.dot(h, bottom, preferred_element_type=f32) + jnp.dot(h, middle, preferred_element_type=f32)
    update = update + jnp.dot(h, top, preferred_element_type=f32)
    result[...] = (update * (by_col * 64.0)).astype(bf16)
    for k, out in enumerate((o0, o1, o2, o3)):
        at = pl.multiple_of(((meta[ZH_AT] + k) & 3) * HALF, HALF)
        out[...] = result[pl.ds(at, HALF), :]


def place_heads(meta, p0, p1, p2, p3, q0, q1, q2, q3, out):
    ylo = meta[Y_AT] & 1
    for dx in range(4):
        for dzh in range(4):
            slot = ((meta[X_AT] - dx) & 3) * 4 + ((meta[ZH_AT] - dzh) & 3)
            for j in range(2):
                at = pl.multiple_of(meta[PERM_AT + slot * 2 + j] * HEAD, HEAD)
                for low, ref in ((ylo, (p0, p1, p2, p3)[dx]), (1 - ylo, (q0, q1, q2, q3)[dx])):
                    rows = pl.ds(pl.multiple_of(low * HALF, HALF), HALF)
                    out[rows, pl.ds(at, HEAD)] = ref[dzh, :, j * HEAD : (j + 1) * HEAD].astype(f32)


Y_INDEX = (0, 2, 1, 3)


def move_x(a, k):
    return lax.ppermute(a, "x", [(i, (i + k) % 4) for i in range(4)])


def move_y(a, k):
    return lax.ppermute(a, ("ylo", "yhi"), [(Y_INDEX[i], Y_INDEX[(i + k) % 4]) for i in range(4)])


def swap_y(a):
    return lax.ppermute(a, "ylo", [(0, 1), (1, 0)])


def swap_core(a):
    return lax.ppermute(a, "core", [(0, 1), (1, 0)])


def swap_z(a):
    return lax.ppermute(a, "z0", [(0, 1), (1, 0)])


def move_z(a, kh, k0):
    pairs = [(h * 2 + l, ((h + kh) % 4) * 2 + (l ^ k0)) for h in range(4) for l in range(2)]
    return lax.ppermute(a, ("zh", "z0"), pairs)


def on_device(activations, cotangent, masked, ratios, owners):
    tok, width = activations.shape
    meta = scalars(owners)
    weight = (masked.astype(f32) * 1000.0 / ratios[0].astype(f32))[:, None]
    blocks = local_kernel(
        prepare,
        [shape((BLOCK, tok), bf16)] * 4 + [shape((tok, BLOCK), bf16)] * 4,
        (meta, activations, cotangent, weight),
        24,
        2 * tok * width,
        "prepare",
    )
    rows, cols = blocks[:4], blocks[4:]
    rows = [rows[0]] + [move_y(rows[k], k) for k in (1, 2, 3)]
    cols = [cols[0]] + [move_x(cols[k], k) for k in (1, 2, 3)]
    r0, g0 = jnp.stack(rows), jnp.stack(cols)
    r1, r3 = move_x(r0, 1), move_x(r0, -1)
    g1, g3 = move_y(g0, 1), move_y(g0, -1)
    r2a, r2b = move_x(r1[:2], 1), move_x(r3[2:], -1)
    g2a, g2b = move_y(g1[:2], 1), move_y(g3[2:], -1)
    keep, send = local_kernel(
        multiply,
        [shape((8, 256, SLOT), bf16)] * 2,
        (meta, r0, r1, r3, r2a, r2b, g0, g1, g3, g2a, g2b),
        40,
        2 * BLOCK * BLOCK * 16 * tok,
        "multiply",
    )
    parts = local_kernel(
        add_cores,
        [shape((256, SLOT), bf16)] * 8,
        (meta, keep, swap_core(send)),
        8,
        8 * 256 * SLOT,
        "add_cores",
    )
    terms = [parts[0]] + [move_z(parts[k0 * 4 + kh], kh, k0) for kh, k0 in ((2, 0), (2, 1), (1, 1), (3, 1), (1, 0), (3, 0), (0, 1))]
    head_grad, mine, other, _ = local_kernel(
        gram_part,
        [shape((256, SLOT), bf16), shape((HEAD, SLOT), f32), shape((HEAD, SLOT), f32), shape((SLOT, SLOT), f32)],
        (meta, *terms),
        8,
        2 * 256 * SLOT * SLOT,
        "gram_part",
    )
    mine = mine + swap_core(other)
    mine = mine + swap_z(mine)
    mine = (mine + move_y(mine, 2)) + (move_y(mine, 1) + move_y(mine, 3))
    update = local_kernel(
        newton,
        [shape((HALF, SLOT), bf16)] * 4 + [shape((256, SLOT), bf16)],
        (meta, mine, swap_core(mine), head_grad),
        16,
        20 * 2 * SLOT**3 * 6,
        "newton",
    )
    p0 = jnp.stack([update[0]] + [lax.ppermute(update[k], "zh", [(i, (i + k) % 4) for i in range(4)]) for k in (1, 2, 3)])
    q0 = swap_y(p0)
    ps = [p0] + [move_x(p0, k) for k in (1, 2, 3)]
    qs = [q0] + [move_x(q0, k) for k in (1, 2, 3)]
    (out,) = local_kernel(
        place_heads, [shape((2 * HALF, width), f32)], (meta, *ps, *qs), 12, 0, "place_heads"
    )
    return out


def solution(mesh):
    axes = ("x", "ylo", "yhi", "zh", "z0", "core")
    fine = Mesh(mesh.devices.reshape(4, 2, 2, 4, 2, 2), axes)
    everywhere = P(axes)
    placed = (P(axes, None), P(axes, None), everywhere, everywhere, P())
    return jax.shard_map(
        on_device,
        mesh=fine,
        in_specs=placed,
        out_specs=P(("yhi", "zh", "z0", "core"), None),
        check_vma=False,
    )
```

```python
import functools

import jax
import jax.numpy as jnp
from jax import lax
from jax.experimental import pallas as pl
from jax.experimental.pallas import tpu as pltpu
from jax.sharding import Mesh
from jax.sharding import PartitionSpec as P

HEADS = 32
NS_ITERS = 5
quintic_a = 3.4445
quintic_b = -4.775
quintic_c = 2.0315
epsilon = 1e-07

PAIRS_AT, PERM_AT = 0, 8

HEAD = 128
SLOT = 2 * HEAD
BLOCK = 1024
HALF = 64
GRAM = HEAD + HALF

f32, bf16 = jnp.float32, jnp.bfloat16


def smem():
    return pl.BlockSpec(memory_space=pltpu.SMEM)


def vmem():
    return pl.BlockSpec(memory_space=pltpu.VMEM)


def anywhere():
    return pl.BlockSpec(memory_space=pl.ANY)


def local_kernel(body, outs, operands, mib, flops, name, in_specs=None, out_specs=None, scratch=()):
    moved = sum(o.size * o.dtype.itemsize for o in list(outs) + list(operands))
    return pl.pallas_call(
        body,
        out_shape=outs,
        in_specs=in_specs or [vmem()] * len(operands),
        out_specs=out_specs or [vmem()] * len(outs),
        scratch_shapes=list(scratch),
        compiler_params=pltpu.CompilerParams(vmem_limit_bytes=mib * 2**20),
        cost_estimate=pl.CostEstimate(flops=flops, bytes_accessed=moved, transcendentals=0),
        name=name,
    )(*operands)


def shape(dims, dtype):
    return jax.ShapeDtypeStruct(dims, dtype)


def y_place():
    return lax.axis_index("yhi") * 2 + lax.axis_index("ylo")


def prepare(owners, ratio, masked, act_far, cot_far, *refs):
    rows_out, cols_out, meta = refs[:4], refs[4:8], refs[8]
    act, cot, count, taken, sems = refs[9:]
    get_act = pltpu.make_async_copy(act_far, act, sems.at[0])
    get_cot = pltpu.make_async_copy(cot_far, cot, sems.at[1])
    get_act.start()
    get_cot.start()

    for v in range(HEADS):
        count[v] = 0
        taken[v] = 0
    for h in range(HEADS):
        count[owners[h]] = count[owners[h]] + 1
    in_pairs = jnp.int32(0)
    for v in range(HEADS):
        in_pairs = in_pairs + jnp.where(count[v] > 1, 2, 0)
    next_pair, next_alone = jnp.int32(0), in_pairs
    for i in range(PERM_AT):
        meta[i] = in_pairs // 2
    for h in range(HEADS):
        owner = owners[h]
        paired = count[owner] > 1
        seen = taken[owner]
        opens = jnp.logical_and(paired, seen == 0)
        place = jnp.where(paired, jnp.where(seen == 0, next_pair, seen), next_alone)
        taken[owner] = place + 1
        meta[PERM_AT + place] = h
        next_pair = next_pair + jnp.where(opens, 2, 0)
        next_alone = next_alone + jnp.where(paired, 0, 1)

    tok, width = act.shape
    here_y, z0, core = y_place(), lax.axis_index("z0"), lax.axis_index("core")
    get_act.wait()
    for k in range(4):
        y = (here_y + k) & 3
        base = (y >> 1) * (width // 2)
        low = (y & 1) * HALF
        for crel in range(2):
            for zrel in range(2):
                for zh in range(4):
                    block = zh * 4 + (z0 ^ zrel) * 2 + (core ^ crel)
                    at = pl.multiple_of(base + block * 128, 128)
                    turned = act[:, pl.ds(at, 128)].T
                    part = jnp.where(low == 0, turned[:HALF], turned[HALF:])
                    to = ((crel * 2 + zrel) * 4 + zh) * HALF
                    rows_out[k][to : to + HALF, :] = part
    along = masked[...].astype(f32) * 1000.0 / ratio[0].astype(f32)
    line = lax.broadcasted_iota(jnp.int32, (tok, tok), 0)
    lane = lax.broadcasted_iota(jnp.int32, (tok, tok), 1)
    weight = jnp.sum(jnp.where(line == lane, along, 0.0), axis=1, keepdims=True)
    get_cot.wait()
    for k in range(4):
        x = (lax.axis_index("x") + k) & 3
        for j in range(8):
            slot = x * 4 + ((lax.axis_index("zh") + j // 2) & 3)
            head = meta[PERM_AT + slot * 2 + j % 2]
            at = pl.multiple_of(head * HEAD, HEAD)
            piece = cot[:, pl.ds(at, HEAD)].astype(f32) * weight
            cols_out[k][:, j * HEAD : (j + 1) * HEAD] = piece.astype(bf16)


def multiply(offset, r0, r1, r3, r2a, r2b, g0, g1, g3, g2a, g2b, out):
    z0 = lax.axis_index("z0")
    half = BLOCK // 2

    def rows_of(dx, dy):
        ref, i = ((r2a if dy < 2 else r2b), dy % 2) if dx == 2 else ({0: r0, 1: r1, 3: r3}[dx], dy)
        return ref[i, offset : offset + half, :]

    def cols_of(dx, dy, at):
        ref, i = ((g2a if dx < 2 else g2b), dx % 2) if dy == 2 else ({0: g0, 1: g1, 3: g3}[dy], dx)
        return ref[i, :, at : at + SLOT]

    for n in range(BLOCK // SLOT):
        total = jnp.zeros((half, SLOT), f32)
        for dx in range(4):
            left = jnp.concatenate([rows_of(dx, dy) for dy in range(4)], axis=1)
            right = jnp.concatenate([cols_of(dx, dy, n * SLOT) for dy in range(4)], axis=0)
            total = total + jnp.dot(left, right, preferred_element_type=f32)
        total = total.astype(bf16)
        out[2 * n] = total[:128]
        out[2 * n + 1] = total[128:256]
        out[8 + ((n - z0) & 3)] = total[256:384]
        out[12 + ((n + 1 - z0) & 3)] = total[384:]


def add_odd(mine, other, up, down):
    for j in range(4):
        up[j] = (mine[8 + j].astype(f32) + other[8 + j].astype(f32)).astype(bf16)
        down[j] = (mine[12 + j].astype(f32) + other[12 + j].astype(f32)).astype(bf16)


def add_even(mine, other, up, down, *outs):
    for a, out in enumerate(outs):
        for h, ref in enumerate((up, down)):
            total = mine[2 * a + h].astype(f32) + other[2 * a + h].astype(f32) + ref[a].astype(f32)
            out[h * 128 : (h + 1) * 128, :] = total.astype(out.dtype)


def gram_part(t0, t1, t2, t3, head_grad, keep, send):
    total = (t0[...] + t1[...].astype(f32)) + (t2[...].astype(f32) + t3[...].astype(f32))
    part = total.astype(bf16)
    head_grad[...] = part
    gram = lax.dot_general(part, part, (((0,), (0,)), ((), ())), preferred_element_type=f32)
    first = jnp.concatenate([gram[:HEAD, :HEAD], gram[:HALF, HEAD:]], axis=0)
    second = jnp.concatenate([gram[HEAD:, HEAD:], gram[HALF:HEAD, HEAD:]], axis=0)
    core = lax.axis_index("core")
    keep[...] = jnp.where(core == 0, first, second)
    send[...] = jnp.where(core == 0, second, first)


def split(a):
    top = a.astype(bf16)
    rest = a - top.astype(f32)
    middle = rest.astype(bf16)
    return top, middle, (rest - middle.astype(f32)).astype(bf16)


def dot(a, b):
    left = jnp.concatenate([a[2], a[0], a[1], a[1], a[0], a[0]], axis=1)
    right = jnp.concatenate([b[0], b[2], b[1], b[0], b[1], b[0]], axis=0)
    return jnp.dot(left, right, preferred_element_type=f32)


def newton(meta, mine, other, head_grad, o0, o1, o2, o3, result):
    core = lax.axis_index("core")
    a, b = mine[...], other[...]
    first, second = jnp.where(core == 0, a, b), jnp.where(core == 0, b, a)
    corner = jnp.concatenate([first[HEAD:], second[HEAD:]], axis=0)
    gram = jnp.concatenate(
        [
            jnp.concatenate([first[:HEAD], corner], axis=1),
            jnp.concatenate([corner.T, second[:HEAD]], axis=1),
        ],
        axis=0,
    )
    zh = lax.axis_index("zh")
    pair = lax.axis_index("x") * 4 + zh < meta[PAIRS_AT]
    row = lax.broadcasted_iota(jnp.int32, (SLOT, SLOT), 0)
    col = lax.broadcasted_iota(jnp.int32, (SLOT, SLOT), 1)
    together = jnp.logical_or((row < HEAD) == (col < HEAD), pair)
    gram = jnp.where(together, gram, 0.0)
    on_diagonal = jnp.where(row == col, gram, 0.0)
    down = jnp.sum(on_diagonal, axis=0, keepdims=True)
    across = jnp.sum(on_diagonal, axis=1, keepdims=True)
    lane, line = col[:1, :], row[:, :1]

    def factor(squares, at, axis):
        low = jnp.sum(jnp.where(at < HEAD, squares, 0.0), axis=axis, keepdims=True)
        high = jnp.sum(jnp.where(at < HEAD, 0.0, squares), axis=axis, keepdims=True)
        norm = jnp.where(pair, low + high, jnp.where(at < HEAD, low, high))
        return 1.0 / (jnp.sqrt(norm) + epsilon)

    by_col = factor(down, lane, 1)
    by_row = factor(across, line, 0)
    gram = gram * by_row * by_col
    unit = jnp.where(row == col, 1.0, 0.0)
    product = None
    for turn in range(NS_ITERS):
        terms = split(gram)
        step = quintic_a * unit + quintic_b * gram + quintic_c * dot(terms, terms)
        by_step = split(step)
        if turn == 0:
            gram = dot(split(dot(terms, by_step)), by_step)
            product = step
        elif turn < NS_ITERS - 1:
            both = jnp.concatenate([product, dot(terms, by_step)], axis=0)
            both = dot(split(both), by_step)
            product, gram = both[:SLOT], both[SLOT:]
        else:
            product = dot(split(product), by_step)
    top, middle, bottom = split(product)
    h = head_grad[...]
    update = jnp.dot(h, bottom, preferred_element_type=f32) + jnp.dot(h, middle, preferred_element_type=f32)
    update = update + jnp.dot(h, top, preferred_element_type=f32)
    result[...] = (update * (by_col * 64.0)).astype(bf16)
    for k, out in enumerate((o0, o1, o2, o3)):
        at = pl.multiple_of(((zh + k) & 3) * HALF, HALF)
        out[...] = result[pl.ds(at, HALF), :]


def place_heads(meta, p0, p1, p2, p3, q0, q1, q2, q3, out):
    ylo, x, zh = lax.axis_index("ylo"), lax.axis_index("x"), lax.axis_index("zh")
    for dx in range(4):
        for dzh in range(4):
            slot = ((x - dx) & 3) * 4 + ((zh - dzh) & 3)
            for j in range(2):
                at = pl.multiple_of(meta[PERM_AT + slot * 2 + j] * HEAD, HEAD)
                for low, ref in ((ylo, (p0, p1, p2, p3)[dx]), (1 - ylo, (q0, q1, q2, q3)[dx])):
                    rows = pl.ds(pl.multiple_of(low * HALF, HALF), HALF)
                    out[rows, pl.ds(at, HEAD)] = ref[dzh, :, j * HEAD : (j + 1) * HEAD].astype(f32)


Y_INDEX = (0, 2, 1, 3)


def move_x(a, k):
    return lax.ppermute(a, "x", [(i, (i + k) % 4) for i in range(4)])


def move_y(a, k):
    return lax.ppermute(a, ("ylo", "yhi"), [(Y_INDEX[i], Y_INDEX[(i + k) % 4]) for i in range(4)])


def move_z(a, k):
    return lax.ppermute(a, ("zh", "z0"), [(i, (i + k) % 8) for i in range(8)])


def swap(a, axis):
    return lax.ppermute(a, axis, [(0, 1), (1, 0)])


def on_device(activations, cotangent, masked, ratios, owners):
    tok, width = activations.shape
    *blocks, meta = local_kernel(
        prepare,
        [shape((BLOCK, tok), bf16)] * 4 + [shape((tok, BLOCK), bf16)] * 4 + [shape((PERM_AT + HEADS,), jnp.int32)],
        (owners, ratios, masked[None, :], activations, cotangent),
        16,
        2 * tok * width,
        "prepare",
        in_specs=[smem(), smem(), vmem(), anywhere(), anywhere()],
        out_specs=[vmem()] * 8 + [smem()],
        scratch=[
            pltpu.VMEM((tok, width), bf16),
            pltpu.VMEM((tok, width), bf16),
            pltpu.SMEM((HEADS,), jnp.int32),
            pltpu.SMEM((HEADS,), jnp.int32),
            pltpu.SemaphoreType.DMA((2,)),
        ],
    )
    rows, cols = blocks[:4], blocks[4:]
    rows = [rows[0]] + [move_y(rows[k], k) for k in (1, 2, 3)]
    cols = [cols[0]] + [move_x(cols[k], k) for k in (1, 2, 3)]
    r0, g0 = jnp.stack(rows), jnp.stack(cols)
    r1, r3 = move_x(r0, 1), move_x(r0, -1)
    g1, g3 = move_y(g0, 1), move_y(g0, -1)
    r2a, r2b = move_x(r1[:2], 1), move_x(r3[2:], -1)
    g2a, g2b = move_y(g1[:2], 1), move_y(g3[2:], -1)
    gathered = (r0, r1, r3, r2a, r2b, g0, g1, g3, g2a, g2b)

    def product(offset, name):
        (out,) = local_kernel(
            functools.partial(multiply, offset),
            [shape((16, 128, SLOT), bf16)],
            gathered,
            32,
            BLOCK * BLOCK * 16 * tok,
            name,
        )
        return out

    send = product(BLOCK // 2, "multiply_other")
    other = swap(send, "core")
    keep = product(0, "multiply_own")
    half_chunks = shape((4, 128, SLOT), bf16)
    up, down = local_kernel(
        add_odd, [half_chunks] * 2, (keep, other), 8, 8 * 128 * SLOT, "add_odd"
    )
    up, down = move_z(up, 1), move_z(down, -1)
    t0, t1, t2, t3 = local_kernel(
        add_even,
        [shape((256, SLOT), f32)] + [shape((256, SLOT), bf16)] * 3,
        (keep, other, up, down),
        8,
        16 * 128 * SLOT,
        "add_even",
    )
    head_grad, mine, theirs = local_kernel(
        gram_part,
        [shape((256, SLOT), bf16), shape((GRAM, HEAD), f32), shape((GRAM, HEAD), f32)],
        (t0, move_z(t1, 2), move_z(t2, 4), move_z(t3, 6)),
        8,
        2 * 256 * SLOT * SLOT,
        "gram_part",
    )
    mine = mine + swap(theirs, "core")
    mine = mine + swap(mine, "z0")
    mine = (mine + move_y(mine, 2)) + (move_y(mine, 1) + move_y(mine, 3))
    update = local_kernel(
        newton,
        [shape((HALF, SLOT), bf16)] * 4 + [shape((256, SLOT), bf16)],
        (meta, mine, swap(mine, "core"), head_grad),
        16,
        20 * 2 * SLOT**3 * 6,
        "newton",
        in_specs=[smem()] + [vmem()] * 3,
    )
    ring = lambda a, k: lax.ppermute(a, "zh", [(i, (i + k) % 4) for i in range(4)])
    p0 = jnp.stack([update[0]] + [ring(update[k], k) for k in (1, 2, 3)])
    q0 = swap(p0, "ylo")
    ps = [p0] + [move_x(p0, k) for k in (1, 2, 3)]
    qs = [q0] + [move_x(q0, k) for k in (1, 2, 3)]
    (out,) = local_kernel(
        place_heads,
        [shape((2 * HALF, width), f32)],
        (meta, *ps, *qs),
        12,
        0,
        "place_heads",
        in_specs=[smem()] + [vmem()] * 8,
    )
    return out


def solution(mesh):
    axes = ("x", "ylo", "yhi", "zh", "z0", "core")
    fine = Mesh(mesh.devices.reshape(4, 2, 2, 4, 2, 2), axes)
    everywhere = P(axes)
    placed = (P(axes, None), P(axes, None), everywhere, everywhere, P())
    return jax.shard_map(
        on_device,
        mesh=fine,
        in_specs=placed,
        out_specs=P(("yhi", "zh", "z0", "core"), None),
        check_vma=False,
    )
```

```python
import functools

import jax
import jax.numpy as jnp
from jax import lax
from jax.experimental import pallas as pl
from jax.experimental.pallas import tpu as pltpu
from jax.sharding import Mesh
from jax.sharding import PartitionSpec as P

HEADS = 32
NS_ITERS = 5
quintic_a = 3.4445
quintic_b = -4.775
quintic_c = 2.0315
epsilon = 1e-07

PAIRS_AT, PERM_AT = 0, 8

HEAD = 128
SLOT = 2 * HEAD
BLOCK = 1024
HALF = 64
GRAM = HEAD + HALF

PREPARE_MIB = 56

f32, bf16 = jnp.float32, jnp.bfloat16


def smem():
    return pl.BlockSpec(memory_space=pltpu.SMEM)


def vmem():
    return pl.BlockSpec(memory_space=pltpu.VMEM)


def anywhere():
    return pl.BlockSpec(memory_space=pl.ANY)


def local_kernel(body, outs, operands, mib, flops, name, in_specs=None, out_specs=None, scratch=()):
    moved = sum(o.size * o.dtype.itemsize for o in list(outs) + list(operands))
    return pl.pallas_call(
        body,
        out_shape=outs,
        in_specs=in_specs or [vmem()] * len(operands),
        out_specs=out_specs or [vmem()] * len(outs),
        scratch_shapes=list(scratch),
        compiler_params=pltpu.CompilerParams(vmem_limit_bytes=mib * 2**20),
        cost_estimate=pl.CostEstimate(flops=flops, bytes_accessed=moved, transcendentals=0),
        name=name,
    )(*operands)


def shape(dims, dtype):
    return jax.ShapeDtypeStruct(dims, dtype)


def y_place():
    return lax.axis_index("yhi") * 2 + lax.axis_index("ylo")


def gray(place):
    return place ^ (place >> 1)


def partner(place, core, i):
    flip = jnp.where(core == 0, i, (i >> 1) | ((i & 1) << 1))
    return gray(gray(place) ^ flip)


def prepare(owners_far, ratio_far, masked, act_far, cot_far, *refs):
    rows_out, cols_out, meta = refs[:2], refs[2:4], refs[4]
    act, cot, owners, ratio, count, taken, sems = refs[5:]
    copies = [
        pltpu.make_async_copy(far, near, sems.at[i])
        for i, (far, near) in enumerate(
            ((owners_far, owners), (ratio_far, ratio), (act_far, act), (cot_far, cot))
        )
    ]
    for copy in copies:
        copy.start()
    for v in range(HEADS):
        count[v] = 0
        taken[v] = 0
    copies[0].wait()

    for h in range(HEADS):
        count[owners[h]] = count[owners[h]] + 1
    in_pairs = jnp.int32(0)
    for v in range(HEADS):
        in_pairs = in_pairs + jnp.where(count[v] > 1, 2, 0)
    next_pair, next_alone = jnp.int32(0), in_pairs
    for i in range(PERM_AT):
        meta[i] = in_pairs // 2
    for h in range(HEADS):
        owner = owners[h]
        paired = count[owner] > 1
        seen = taken[owner]
        opens = jnp.logical_and(paired, seen == 0)
        place = jnp.where(paired, jnp.where(seen == 0, next_pair, seen), next_alone)
        taken[owner] = place + 1
        meta[PERM_AT + place] = h
        next_pair = next_pair + jnp.where(opens, 2, 0)
        next_alone = next_alone + jnp.where(paired, 0, 1)

    tok, width = act.shape
    here_y, z0, core = y_place(), lax.axis_index("z0"), lax.axis_index("core")
    copies[1].wait()
    copies[2].wait()
    for i in range(4):
        y = partner(here_y, core, i)
        base = (y >> 1) * (width // 2)
        low = (y & 1) * HALF
        for crel in range(2):
            for zrel in range(2):
                for zh in range(4):
                    block = zh * 4 + (z0 ^ zrel) * 2 + (core ^ crel)
                    at = pl.multiple_of(base + block * 128, 128)
                    turned = act[:, pl.ds(at, 128)].T
                    part = jnp.where(low == 0, turned[:HALF], turned[HALF:])
                    to = ((crel * 2 + zrel) * 4 + zh) * HALF
                    rows_out[i & 1][i >> 1, to : to + HALF, :] = part
    along = masked[...].astype(f32) * 1000.0 / ratio[0].astype(f32)
    line = lax.broadcasted_iota(jnp.int32, (tok, tok), 0)
    lane = lax.broadcasted_iota(jnp.int32, (tok, tok), 1)
    weight = jnp.sum(jnp.where(line == lane, along, 0.0), axis=1, keepdims=True)
    copies[3].wait()
    for i in range(4):
        x = partner(lax.axis_index("x"), core, i)
        for j in range(8):
            slot = x * 4 + ((lax.axis_index("zh") + j // 2) & 3)
            head = meta[PERM_AT + slot * 2 + j % 2]
            at = pl.multiple_of(head * HEAD, HEAD)
            piece = cot[:, pl.ds(at, HEAD)].astype(f32) * weight
            cols_out[i & 1][i >> 1, :, j * HEAD : (j + 1) * HEAD] = piece.astype(bf16)


def multiply(other_core, *refs):
    rows, cols, out = refs[:4], refs[4:8], refs[8]
    z0, core = lax.axis_index("z0"), lax.axis_index("core") ^ other_core
    half = BLOCK // 2
    offset = other_core * half
    for n in range(BLOCK // SLOT):
        total = jnp.zeros((half, SLOT), f32)
        for i in range(4):
            left = jnp.concatenate([rows[i][j, offset : offset + half, :] for j in range(4)], axis=1)
            right = jnp.concatenate([cols[j][i, :, n * SLOT : (n + 1) * SLOT] for j in range(4)], axis=0)
            total = total + jnp.dot(left, right, preferred_element_type=f32)
        total = total.astype(bf16)
        out[jnp.where(core == 0, n, -n) & 3] = total[:256]
        out[4 + (jnp.where(core == 0, n - z0, z0 - n - 1) & 3)] = total[256:]


def add_odd(mine, other, out):
    for j in range(4):
        out[j] = (mine[4 + j].astype(f32) + other[4 + j].astype(f32)).astype(bf16)


def add_even(mine, other, arrived, stay, move):
    for a in range(4):
        total = mine[a].astype(f32) + other[a].astype(f32) + arrived[a].astype(f32)
        if a % 2:
            move[a // 2] = total.astype(bf16)
        else:
            stay[a // 2] = total


def add_far(stay, arrived, near, far):
    near[...] = stay[0] + arrived[0].astype(f32)
    far[...] = (stay[1] + arrived[1].astype(f32)).astype(bf16)


def gram_part(near, arrived, head_grad, keep, send):
    part = (near[...] + arrived[...].astype(f32)).astype(bf16)
    head_grad[...] = part
    gram = lax.dot_general(part, part, (((0,), (0,)), ((), ())), preferred_element_type=f32)
    first = jnp.concatenate([gram[:HEAD, :HEAD], gram[:HALF, HEAD:]], axis=0)
    second = jnp.concatenate([gram[HEAD:, HEAD:], gram[HALF:HEAD, HEAD:]], axis=0)
    core = lax.axis_index("core")
    keep[...] = jnp.where(core == 0, first, second)
    send[...] = jnp.where(core == 0, second, first)


def product(a, b):
    return jnp.dot(a, b, precision=lax.Precision.HIGHEST, preferred_element_type=f32)


def two_terms(a):
    top = a.astype(bf16)
    return top, (a - top.astype(f32)).astype(bf16)


def short_product(a, b):
    dot = functools.partial(jnp.dot, preferred_element_type=f32)
    return (dot(a[1], b[0]) + dot(a[0], b[1])) + dot(a[0], b[0])


def newton(meta, mine, other, head_grad, keep, send, result):
    core = lax.axis_index("core")
    a, b = mine[...], other[...]
    first, second = jnp.where(core == 0, a, b), jnp.where(core == 0, b, a)
    corner = jnp.concatenate([first[HEAD:], second[HEAD:]], axis=0)
    gram = jnp.concatenate(
        [
            jnp.concatenate([first[:HEAD], corner], axis=1),
            jnp.concatenate([corner.T, second[:HEAD]], axis=1),
        ],
        axis=0,
    )
    zh = lax.axis_index("zh")
    pair = lax.axis_index("x") * 4 + zh < meta[PAIRS_AT]
    row = lax.broadcasted_iota(jnp.int32, (SLOT, SLOT), 0)
    col = lax.broadcasted_iota(jnp.int32, (SLOT, SLOT), 1)
    together = jnp.logical_or((row < HEAD) == (col < HEAD), pair)
    gram = jnp.where(together, gram, 0.0)
    on_diagonal = jnp.where(row == col, gram, 0.0)
    down = jnp.sum(on_diagonal, axis=0, keepdims=True)
    across = jnp.sum(on_diagonal, axis=1, keepdims=True)
    lane, line = col[:1, :], row[:, :1]

    def factor(squares, at, axis):
        low = jnp.sum(jnp.where(at < HEAD, squares, 0.0), axis=axis, keepdims=True)
        high = jnp.sum(jnp.where(at < HEAD, 0.0, squares), axis=axis, keepdims=True)
        norm = jnp.where(pair, low + high, jnp.where(at < HEAD, low, high))
        return 1.0 / (jnp.sqrt(norm) + epsilon)

    by_col = factor(down, lane, 1)
    by_row = factor(across, line, 0)
    gram = gram * by_row * by_col
    unit = jnp.where(row == col, 1.0, 0.0)
    factors = None
    for turn in range(NS_ITERS):
        multiplied = product if turn < 2 else lambda p, q: short_product(two_terms(p), two_terms(q))
        step = quintic_a * unit + quintic_b * gram + quintic_c * multiplied(gram, gram)
        if turn < NS_ITERS - 1:
            gram = multiplied(multiplied(gram, step), step)
        factors = step if factors is None else product(factors, step)
    top, middle = two_terms(factors)
    bottom = (factors - top.astype(f32) - middle.astype(f32)).astype(bf16)
    h = head_grad[...]
    update = jnp.dot(h, bottom, preferred_element_type=f32) + jnp.dot(h, middle, preferred_element_type=f32)
    update = update + jnp.dot(h, top, preferred_element_type=f32)
    result[...] = (update * (by_col * 64.0)).astype(bf16)
    for i in range(4):
        at = pl.multiple_of(partner(zh, core, i) * HALF, HALF)
        (send if i & 1 else keep)[i >> 1] = result[pl.ds(at, HALF), :]


def place_heads(meta, p0, p1, p2, p3, q0, q1, q2, q3, out):
    ylo, x, zh = lax.axis_index("ylo"), lax.axis_index("x"), lax.axis_index("zh")
    core = lax.axis_index("core")
    for dx in range(4):
        for i in range(4):
            slot = ((x - dx) & 3) * 4 + partner(zh, core, i)
            for j in range(2):
                at = pl.multiple_of(meta[PERM_AT + slot * 2 + j] * HEAD, HEAD)
                for low, ref in ((ylo, (p0, p1, p2, p3)[dx]), (1 - ylo, (q0, q1, q2, q3)[dx])):
                    rows = pl.ds(pl.multiple_of(low * HALF, HALF), HALF)
                    out[rows, pl.ds(at, HEAD)] = ref[i, :, j * HEAD : (j + 1) * HEAD].astype(f32)


RINGS = {"x": ("x",), "y": ("ylo", "yhi"), "zh": ("zh",)}


def ring_index(ring, place):
    return (place & 1) * 2 + (place >> 1) if ring == "y" else place


def exchange(a, ring, second):
    pairs = []
    for place in range(4):
        for core in range(2):
            to = gray(gray(place) ^ (1 << (core ^ second)))
            pairs.append((ring_index(ring, place) * 2 + core, ring_index(ring, to) * 2 + core))
    return lax.ppermute(a, RINGS[ring] + ("core",), pairs)


def move_x(a, k):
    return lax.ppermute(a, "x", [(i, (i + k) % 4) for i in range(4)])


def move_z(a, k):
    pairs = [(i * 2 + core, (i + (k, -k)[core]) % 8 * 2 + core) for i in range(8) for core in range(2)]
    return lax.ppermute(a, ("zh", "z0", "core"), pairs)


def swap(a, axis):
    return lax.ppermute(a, axis, [(0, 1), (1, 0)])


def each_to_each(keep, send, ring):
    first = exchange(send, ring, 0)
    second = exchange(jnp.stack([keep[1], first[1]]), ring, 1)
    return jnp.stack([keep[0], first[0], second[0], second[1]])


def on_device(activations, cotangent, masked, ratios, owners):
    tok, width = activations.shape
    row_blocks, col_blocks = shape((2, BLOCK, tok), bf16), shape((2, tok, BLOCK), bf16)
    keep_r, send_r, keep_g, send_g, meta = local_kernel(
        prepare,
        [row_blocks, row_blocks, col_blocks, col_blocks, shape((PERM_AT + HEADS,), jnp.int32)],
        (owners, ratios, masked[None, :], activations, cotangent),
        PREPARE_MIB,
        2 * tok * width,
        "prepare",
        in_specs=[anywhere(), anywhere(), vmem(), anywhere(), anywhere()],
        out_specs=[vmem()] * 4 + [smem()],
        scratch=[
            pltpu.VMEM((tok, width), bf16),
            pltpu.VMEM((tok, width), bf16),
            pltpu.SMEM((HEADS,), jnp.int32),
            pltpu.SMEM((1,), jnp.int32),
            pltpu.SMEM((HEADS,), jnp.int32),
            pltpu.SMEM((HEADS,), jnp.int32),
            pltpu.SemaphoreType.DMA((4,)),
        ],
    )
    r0, g0 = each_to_each(keep_r, send_r, "y"), each_to_each(keep_g, send_g, "x")
    r1, r2 = exchange(r0, "x", 0), exchange(r0, "x", 1)
    g1, g2 = exchange(g0, "y", 0), exchange(g0, "y", 1)
    r3, g3 = exchange(r1, "x", 1), exchange(g1, "y", 1)
    gathered = (r0, r1, r2, r3, g0, g1, g2, g3)

    def part(other_core, name):
        (out,) = local_kernel(
            functools.partial(multiply, other_core),
            [shape((8, 256, SLOT), bf16)],
            gathered,
            32,
            BLOCK * BLOCK * 16 * tok,
            name,
        )
        return out

    other = swap(part(1, "multiply_other"), "core")
    own = part(0, "multiply_own")
    (odd,) = local_kernel(add_odd, [shape((4, 256, SLOT), bf16)], (own, other), 8, 4 * 256 * SLOT, "add_odd")
    stay, move = local_kernel(
        add_even,
        [shape((2, 256, SLOT), f32), shape((2, 256, SLOT), bf16)],
        (own, other, move_z(odd, 1)),
        8,
        8 * 256 * SLOT,
        "add_even",
    )
    near, far = local_kernel(
        add_far,
        [shape((256, SLOT), f32), shape((256, SLOT), bf16)],
        (stay, move_z(move, 2)),
        8,
        2 * 256 * SLOT,
        "add_far",
    )
    head_grad, mine, theirs = local_kernel(
        gram_part,
        [shape((256, SLOT), bf16), shape((GRAM, HEAD), f32), shape((GRAM, HEAD), f32)],
        (near, move_z(far, 4)),
        8,
        2 * 256 * SLOT * SLOT,
        "gram_part",
    )
    mine = mine + swap(theirs, "core")
    mine = mine + swap(mine, "z0")
    mine = mine + exchange(mine, "y", 0)
    mine = mine + exchange(mine, "y", 1)
    keep, send = local_kernel(
        newton,
        [shape((2, HALF, SLOT), bf16)] * 2,
        (meta, mine, swap(mine, "core"), head_grad),
        16,
        20 * 2 * SLOT**3 * 6,
        "newton",
        in_specs=[smem()] + [vmem()] * 3,
        scratch=[pltpu.VMEM((256, SLOT), bf16)],
    )
    p0 = each_to_each(keep, send, "zh")
    q0 = swap(p0, "ylo")
    ps = [p0] + [move_x(p0, k) for k in (1, 2, 3)]
    qs = [q0] + [move_x(q0, k) for k in (1, 2, 3)]
    (out,) = local_kernel(
        place_heads,
        [shape((2 * HALF, width), f32)],
        (meta, *ps, *qs),
        12,
        0,
        "place_heads",
        in_specs=[smem()] + [vmem()] * 8,
    )
    return out


def solution(mesh):
    axes = ("x", "ylo", "yhi", "zh", "z0", "core")
    fine = Mesh(mesh.devices.reshape(4, 2, 2, 4, 2, 2), axes)
    everywhere = P(axes)
    placed = (P(axes, None), P(axes, None), everywhere, everywhere, P())
    return jax.shard_map(
        on_device,
        mesh=fine,
        in_specs=placed,
        out_specs=P(("yhi", "zh", "z0", "core"), None),
        check_vma=False,
    )
```

```python
import functools

import jax
import jax.numpy as jnp
from jax import lax
from jax.experimental import pallas as pl
from jax.experimental.pallas import tpu as pltpu
from jax.sharding import Mesh
from jax.sharding import PartitionSpec as P

HEADS = 32
NS_ITERS = 5
quintic_a = 3.4445
quintic_b = -4.775
quintic_c = 2.0315
epsilon = 1e-07

PAIRS_AT, PERM_AT = 0, 8

HEAD = 128
SLOT = 2 * HEAD
BLOCK = 1024
HALF = 64
GRAM = HEAD + HALF

PREPARE_MIB = 56

f32, bf16 = jnp.float32, jnp.bfloat16


def smem():
    return pl.BlockSpec(memory_space=pltpu.SMEM)


def vmem():
    return pl.BlockSpec(memory_space=pltpu.VMEM)


def anywhere():
    return pl.BlockSpec(memory_space=pl.ANY)


def local_kernel(body, outs, operands, mib, flops, name, in_specs=None, out_specs=None, scratch=()):
    moved = sum(o.size * o.dtype.itemsize for o in list(outs) + list(operands))
    return pl.pallas_call(
        body,
        out_shape=outs,
        in_specs=in_specs or [vmem()] * len(operands),
        out_specs=out_specs or [vmem()] * len(outs),
        scratch_shapes=list(scratch),
        compiler_params=pltpu.CompilerParams(vmem_limit_bytes=mib * 2**20),
        cost_estimate=pl.CostEstimate(flops=flops, bytes_accessed=moved, transcendentals=0),
        name=name,
    )(*operands)


def shape(dims, dtype):
    return jax.ShapeDtypeStruct(dims, dtype)


def y_place():
    return lax.axis_index("yhi") * 2 + lax.axis_index("ylo")


def prepare(owners_far, ratio_far, masked, act_far, cot_far, *refs):
    rows_out, cols_out, meta = refs[:4], refs[4:8], refs[8]
    act, cot, owners, ratio, count, taken, sems = refs[9:]
    copies = [
        pltpu.make_async_copy(far, near, sems.at[i])
        for i, (far, near) in enumerate(
            ((owners_far, owners), (ratio_far, ratio), (act_far, act), (cot_far, cot))
        )
    ]
    for copy in copies:
        copy.start()
    for v in range(HEADS):
        count[v] = 0
        taken[v] = 0
    copies[0].wait()

    for h in range(HEADS):
        count[owners[h]] = count[owners[h]] + 1
    in_pairs = jnp.int32(0)
    for v in range(HEADS):
        in_pairs = in_pairs + jnp.where(count[v] > 1, 2, 0)
    next_pair, next_alone = jnp.int32(0), in_pairs
    for i in range(PERM_AT):
        meta[i] = in_pairs // 2
    for h in range(HEADS):
        owner = owners[h]
        paired = count[owner] > 1
        seen = taken[owner]
        opens = jnp.logical_and(paired, seen == 0)
        place = jnp.where(paired, jnp.where(seen == 0, next_pair, seen), next_alone)
        taken[owner] = place + 1
        meta[PERM_AT + place] = h
        next_pair = next_pair + jnp.where(opens, 2, 0)
        next_alone = next_alone + jnp.where(paired, 0, 1)

    tok, width = act.shape
    here_y, z0, core = y_place(), lax.axis_index("z0"), lax.axis_index("core")
    copies[1].wait()
    copies[2].wait()
    for k in range(4):
        y = (here_y + k) & 3
        base = (y >> 1) * (width // 2)
        low = (y & 1) * HALF
        for zrel in range(2):
            for crel in range(2):
                for zh in range(4):
                    block = zh * 4 + (z0 ^ zrel) * 2 + (core ^ crel)
                    at = pl.multiple_of(base + block * 128, 128)
                    turned = act[:, pl.ds(at, 128)].T
                    part = jnp.where(low == 0, turned[:HALF], turned[HALF:])
                    to = ((zrel * 2 + crel) * 4 + zh) * HALF
                    rows_out[k][to : to + HALF, :] = part
    along = masked[...].astype(f32) * 1000.0 / ratio[0].astype(f32)
    line = lax.broadcasted_iota(jnp.int32, (tok, tok), 0)
    lane = lax.broadcasted_iota(jnp.int32, (tok, tok), 1)
    weight = jnp.sum(jnp.where(line == lane, along, 0.0), axis=1, keepdims=True)
    copies[3].wait()
    for k in range(4):
        x = (lax.axis_index("x") + k) & 3
        for j in range(8):
            slot = x * 4 + ((lax.axis_index("zh") + j // 2) & 3)
            head = meta[PERM_AT + slot * 2 + j % 2]
            at = pl.multiple_of(head * HEAD, HEAD)
            piece = cot[:, pl.ds(at, HEAD)].astype(f32) * weight
            cols_out[k][:, j * HEAD : (j + 1) * HEAD] = piece.astype(bf16)


def piece(near, opposite, i, j):
    return (opposite[j // 2], j % 2) if i == 2 else (near[i], j)


def operands(refs, pairs, rows, at):
    r0, r1, r3, r2a, r2b, g0, g1, g3, g2a, g2b = refs
    left, right = [], []
    for dx, dy in pairs:
        ref, i = piece({0: r0, 1: r1, 3: r3}, (r2a, r2b), dx, dy)
        left.append(ref[i, rows[0] : rows[1], :])
        ref, i = piece({0: g0, 1: g1, 3: g3}, (g2a, g2b), dy, dx)
        right.append(ref[i, :, at : at + SLOT])
    return jnp.concatenate(left, axis=1), jnp.concatenate(right, axis=0)


def multiply_near(r0, r1, r3, g0, g1, g3, out):
    refs = (r0, r1, r3, None, None, g0, g1, g3, None, None)
    pairs = [(dx, dy) for dx in (0, 1, 3) for dy in (0, 1, 3)]
    for n in range(BLOCK // SLOT):
        left, right = operands(refs, pairs, (0, BLOCK), n * SLOT)
        out[:, n * SLOT : (n + 1) * SLOT] = jnp.dot(left, right, preferred_element_type=f32)


def multiply_rest(odd, near, *refs):
    refs, outs = refs[:10], refs[10:]
    z0 = lax.axis_index("z0")
    half = BLOCK // 2
    rows = (odd * half, (odd + 1) * half)
    pairs = [(dx, dy) for dx in range(4) for dy in range(4) if dx == 2 or dy == 2]
    for n in range(BLOCK // SLOT):
        left, right = operands(refs, pairs, rows, n * SLOT)
        total = near[rows[0] : rows[1], n * SLOT : (n + 1) * SLOT]
        total = (total + jnp.dot(left, right, preferred_element_type=f32)).astype(bf16)
        for out, part in zip(outs, (total[: half // 2], total[half // 2 :])):
            if odd:
                out[(n - z0) & 3] = part[:128]
                out[4 + ((n + 1 - z0) & 3)] = part[128:]
            else:
                out[2 * n] = part[:128]
                out[2 * n + 1] = part[128:]


def add_odd(mine, other, up, down):
    for j in range(4):
        up[j] = (mine[j].astype(f32) + other[j].astype(f32)).astype(bf16)
        down[j] = (mine[4 + j].astype(f32) + other[4 + j].astype(f32)).astype(bf16)


def add_even(mine, other, up, down, *outs):
    for a, out in enumerate(outs):
        for h, ref in enumerate((up, down)):
            total = mine[2 * a + h].astype(f32) + other[2 * a + h].astype(f32) + ref[a].astype(f32)
            out[h * 128 : (h + 1) * 128, :] = total.astype(out.dtype)


def gram_part(t0, t1, t2, t3, head_grad, keep, send):
    total = (t0[...] + t1[...].astype(f32)) + (t2[...].astype(f32) + t3[...].astype(f32))
    part = total.astype(bf16)
    head_grad[...] = part
    gram = lax.dot_general(part, part, (((0,), (0,)), ((), ())), preferred_element_type=f32)
    first = jnp.concatenate([gram[:HEAD, :HEAD], gram[:HALF, HEAD:]], axis=0)
    second = jnp.concatenate([gram[HEAD:, HEAD:], gram[HALF:HEAD, HEAD:]], axis=0)
    core = lax.axis_index("core")
    keep[...] = jnp.where(core == 0, first, second)
    send[...] = jnp.where(core == 0, second, first)


def product(a, b):
    return jnp.dot(a, b, precision=lax.Precision.HIGHEST, preferred_element_type=f32)


def two_terms(a):
    top = a.astype(bf16)
    return top, (a - top.astype(f32)).astype(bf16)


def short_product(a, b):
    dot = functools.partial(jnp.dot, preferred_element_type=f32)
    return (dot(a[1], b[0]) + dot(a[0], b[1])) + dot(a[0], b[0])


def newton(meta, mine, other, head_grad, o0, o1, o2, o3, result):
    core = lax.axis_index("core")
    a, b = mine[...], other[...]
    first, second = jnp.where(core == 0, a, b), jnp.where(core == 0, b, a)
    corner = jnp.concatenate([first[HEAD:], second[HEAD:]], axis=0)
    gram = jnp.concatenate(
        [
            jnp.concatenate([first[:HEAD], corner], axis=1),
            jnp.concatenate([corner.T, second[:HEAD]], axis=1),
        ],
        axis=0,
    )
    zh = lax.axis_index("zh")
    pair = lax.axis_index("x") * 4 + zh < meta[PAIRS_AT]
    row = lax.broadcasted_iota(jnp.int32, (SLOT, SLOT), 0)
    col = lax.broadcasted_iota(jnp.int32, (SLOT, SLOT), 1)
    together = jnp.logical_or((row < HEAD) == (col < HEAD), pair)
    gram = jnp.where(together, gram, 0.0)
    on_diagonal = jnp.where(row == col, gram, 0.0)
    down = jnp.sum(on_diagonal, axis=0, keepdims=True)
    across = jnp.sum(on_diagonal, axis=1, keepdims=True)
    lane, line = col[:1, :], row[:, :1]

    def factor(squares, at, axis):
        low = jnp.sum(jnp.where(at < HEAD, squares, 0.0), axis=axis, keepdims=True)
        high = jnp.sum(jnp.where(at < HEAD, 0.0, squares), axis=axis, keepdims=True)
        norm = jnp.where(pair, low + high, jnp.where(at < HEAD, low, high))
        return 1.0 / (jnp.sqrt(norm) + epsilon)

    by_col = factor(down, lane, 1)
    by_row = factor(across, line, 0)
    gram = gram * by_row * by_col
    unit = jnp.where(row == col, 1.0, 0.0)
    factors = None
    for turn in range(NS_ITERS):
        multiplied = product if turn < 2 else lambda p, q: short_product(two_terms(p), two_terms(q))
        step = quintic_a * unit + quintic_b * gram + quintic_c * multiplied(gram, gram)
        if turn < NS_ITERS - 1:
            gram = multiplied(multiplied(gram, step), step)
        factors = step if factors is None else product(factors, step)
    top, middle = two_terms(factors)
    bottom = (factors - top.astype(f32) - middle.astype(f32)).astype(bf16)
    h = head_grad[...]
    update = jnp.dot(h, bottom, preferred_element_type=f32) + jnp.dot(h, middle, preferred_element_type=f32)
    update = update + jnp.dot(h, top, preferred_element_type=f32)
    result[...] = (update * (by_col * 64.0)).astype(bf16)
    for k, out in enumerate((o0, o1, o2, o3)):
        at = pl.multiple_of(((zh + k) & 3) * HALF, HALF)
        out[...] = result[pl.ds(at, HALF), :]


def place_heads(meta, p0, p1, p2, p3, q0, q1, q2, q3, out):
    ylo, x, zh = lax.axis_index("ylo"), lax.axis_index("x"), lax.axis_index("zh")
    for dx in range(4):
        for dzh in range(4):
            slot = ((x - dx) & 3) * 4 + ((zh - dzh) & 3)
            for j in range(2):
                at = pl.multiple_of(meta[PERM_AT + slot * 2 + j] * HEAD, HEAD)
                for low, ref in ((ylo, (p0, p1, p2, p3)[dx]), (1 - ylo, (q0, q1, q2, q3)[dx])):
                    rows = pl.ds(pl.multiple_of(low * HALF, HALF), HALF)
                    out[rows, pl.ds(at, HEAD)] = ref[dzh, :, j * HEAD : (j + 1) * HEAD].astype(f32)


Y_INDEX = (0, 2, 1, 3)


def move_x(a, k):
    return lax.ppermute(a, "x", [(i, (i + k) % 4) for i in range(4)])


def move_y(a, k):
    return lax.ppermute(a, ("ylo", "yhi"), [(Y_INDEX[i], Y_INDEX[(i + k) % 4]) for i in range(4)])


def move_z(a, k):
    return lax.ppermute(a, ("zh", "z0"), [(i, (i + k) % 8) for i in range(8)])


def swap(a, axis):
    return lax.ppermute(a, axis, [(0, 1), (1, 0)])


def on_device(activations, cotangent, masked, ratios, owners):
    tok, width = activations.shape
    *blocks, meta = local_kernel(
        prepare,
        [shape((BLOCK, tok), bf16)] * 4 + [shape((tok, BLOCK), bf16)] * 4 + [shape((PERM_AT + HEADS,), jnp.int32)],
        (owners, ratios, masked[None, :], activations, cotangent),
        PREPARE_MIB,
        2 * tok * width,
        "prepare",
        in_specs=[anywhere(), anywhere(), vmem(), anywhere(), anywhere()],
        out_specs=[vmem()] * 8 + [smem()],
        scratch=[
            pltpu.VMEM((tok, width), bf16),
            pltpu.VMEM((tok, width), bf16),
            pltpu.SMEM((HEADS,), jnp.int32),
            pltpu.SMEM((1,), jnp.int32),
            pltpu.SMEM((HEADS,), jnp.int32),
            pltpu.SMEM((HEADS,), jnp.int32),
            pltpu.SemaphoreType.DMA((4,)),
        ],
    )
    rows, cols = blocks[:4], blocks[4:]
    rows = [rows[0]] + [move_y(rows[k], k) for k in (1, 2, 3)]
    cols = [cols[0]] + [move_x(cols[k], k) for k in (1, 2, 3)]
    r0, g0 = jnp.stack(rows), jnp.stack(cols)
    r1, r3 = move_x(r0, 1), move_x(r0, -1)
    g1, g3 = move_y(g0, 1), move_y(g0, -1)
    r2a, r2b = move_x(r1[:2], 1), move_x(r3[2:], -1)
    g2a, g2b = move_y(g1[:2], 1), move_y(g3[2:], -1)
    gathered = (r0, r1, r3, r2a, r2b, g0, g1, g3, g2a, g2b)

    flops = 2 * BLOCK * BLOCK * tok
    (near,) = local_kernel(
        multiply_near, [shape((BLOCK, BLOCK), f32)], (r0, r1, r3, g0, g1, g3), 32, 9 * flops, "multiply_near"
    )

    def rest(odd, name):
        return local_kernel(
            functools.partial(multiply_rest, odd),
            [shape((8, 128, SLOT), bf16)] * 2,
            (near, *gathered),
            32,
            7 * flops // 2,
            name,
        )

    own_odd, odd = rest(1, "multiply_odd")
    odd = swap(odd, "core")
    own_even, even = rest(0, "multiply_even")
    even = swap(even, "core")
    half_chunks = shape((4, 128, SLOT), bf16)
    up, down = local_kernel(
        add_odd, [half_chunks] * 2, (own_odd, odd), 8, 8 * 128 * SLOT, "add_odd"
    )
    up, down = move_z(up, 1), move_z(down, -1)
    t0, t1, t2, t3 = local_kernel(
        add_even,
        [shape((256, SLOT), f32)] + [shape((256, SLOT), bf16)] * 3,
        (own_even, even, up, down),
        8,
        16 * 128 * SLOT,
        "add_even",
    )
    head_grad, mine, theirs = local_kernel(
        gram_part,
        [shape((256, SLOT), bf16), shape((GRAM, HEAD), f32), shape((GRAM, HEAD), f32)],
        (t0, move_z(t1, 2), move_z(t2, 4), move_z(t3, 6)),
        8,
        2 * 256 * SLOT * SLOT,
        "gram_part",
    )
    mine = mine + swap(theirs, "core")
    mine = mine + swap(mine, "z0")
    mine = (mine + move_y(mine, 2)) + (move_y(mine, 1) + move_y(mine, 3))
    update = local_kernel(
        newton,
        [shape((HALF, SLOT), bf16)] * 4,
        (meta, mine, swap(mine, "core"), head_grad),
        16,
        20 * 2 * SLOT**3 * 6,
        "newton",
        in_specs=[smem()] + [vmem()] * 3,
        scratch=[pltpu.VMEM((256, SLOT), bf16)],
    )
    ring = lambda a, k: lax.ppermute(a, "zh", [(i, (i + k) % 4) for i in range(4)])
    p0 = jnp.stack([update[0]] + [ring(update[k], k) for k in (1, 2, 3)])
    q0 = swap(p0, "ylo")
    ps = [p0] + [move_x(p0, k) for k in (1, 2, 3)]
    qs = [q0] + [move_x(q0, k) for k in (1, 2, 3)]
    (out,) = local_kernel(
        place_heads,
        [shape((2 * HALF, width), f32)],
        (meta, *ps, *qs),
        12,
        0,
        "place_heads",
        in_specs=[smem()] + [vmem()] * 8,
    )
    return out


def solution(mesh):
    axes = ("x", "ylo", "yhi", "zh", "z0", "core")
    fine = Mesh(mesh.devices.reshape(4, 2, 2, 4, 2, 2), axes)
    everywhere = P(axes)
    placed = (P(axes, None), P(axes, None), everywhere, everywhere, P())
    return jax.shard_map(
        on_device,
        mesh=fine,
        in_specs=placed,
        out_specs=P(("yhi", "zh", "z0", "core"), None),
        check_vma=False,
    )
```

```python
import functools

import jax
import jax.numpy as jnp
from jax import lax
from jax.experimental import pallas as pl
from jax.experimental.pallas import tpu as pltpu
from jax.sharding import Mesh
from jax.sharding import PartitionSpec as P

HEADS = 32
NS_ITERS = 5
quintic_a = 3.4445
quintic_b = -4.775
quintic_c = 2.0315
epsilon = 1e-07

PAIRS_AT, PERM_AT = 0, 8

HEAD = 128
SLOT = 2 * HEAD
BLOCK = 1024
HALF = 64
GRAM = HEAD + HALF

f32, bf16 = jnp.float32, jnp.bfloat16


def smem():
    return pl.BlockSpec(memory_space=pltpu.SMEM)


def vmem():
    return pl.BlockSpec(memory_space=pltpu.VMEM)


def hbm():
    return pl.BlockSpec(memory_space=pltpu.HBM)


def local_kernel(body, outs, operands, mib, flops, name, in_specs=None, out_specs=None, scratch=()):
    moved = sum(o.size * o.dtype.itemsize for o in list(outs) + list(operands))
    return pl.pallas_call(
        body,
        out_shape=outs,
        in_specs=in_specs or [vmem()] * len(operands),
        out_specs=out_specs or [vmem()] * len(outs),
        scratch_shapes=list(scratch),
        compiler_params=pltpu.CompilerParams(vmem_limit_bytes=mib * 2**20),
        cost_estimate=pl.CostEstimate(flops=flops, bytes_accessed=moved, transcendentals=0),
        name=name,
    )(*operands)


def shape(dims, dtype):
    return jax.ShapeDtypeStruct(dims, dtype)


def y_place():
    return lax.axis_index("yhi") * 2 + lax.axis_index("ylo")


def prepare(owners_far, ratio_far, masked, act_far, cot_far, *refs):
    rows_out, cols_out, meta = refs[:4], refs[4:8], refs[8]
    act, cot, owners, ratio, count, taken, sems = refs[9:]
    copies = [
        pltpu.make_async_copy(far, near, sems.at[i])
        for i, (far, near) in enumerate(
            ((owners_far, owners), (ratio_far, ratio), (act_far, act), (cot_far, cot))
        )
    ]
    for copy in copies:
        copy.start()
    for v in range(HEADS):
        count[v] = 0
        taken[v] = 0
    copies[0].wait()

    for h in range(HEADS):
        count[owners[h]] = count[owners[h]] + 1
    in_pairs = jnp.int32(0)
    for v in range(HEADS):
        in_pairs = in_pairs + jnp.where(count[v] > 1, 2, 0)
    next_pair, next_alone = jnp.int32(0), in_pairs
    for i in range(PERM_AT):
        meta[i] = in_pairs // 2
    for h in range(HEADS):
        owner = owners[h]
        paired = count[owner] > 1
        seen = taken[owner]
        opens = jnp.logical_and(paired, seen == 0)
        place = jnp.where(paired, jnp.where(seen == 0, next_pair, seen), next_alone)
        taken[owner] = place + 1
        meta[PERM_AT + place] = h
        next_pair = next_pair + jnp.where(opens, 2, 0)
        next_alone = next_alone + jnp.where(paired, 0, 1)

    tok, width = act.shape
    here_y, z0, core = y_place(), lax.axis_index("z0"), lax.axis_index("core")
    copies[1].wait()
    copies[2].wait()
    for k in range(4):
        y = (here_y + k) & 3
        base = (y >> 1) * (width // 2)
        low = (y & 1) * HALF
        for zrel in range(2):
            for crel in range(2):
                for zh in range(4):
                    block = zh * 4 + (z0 ^ zrel) * 2 + (core ^ crel)
                    at = pl.multiple_of(base + block * 128, 128)
                    turned = act[:, pl.ds(at, 128)].T
                    part = jnp.where(low == 0, turned[:HALF], turned[HALF:])
                    to = ((zrel * 2 + crel) * 4 + zh) * HALF
                    rows_out[k][to : to + HALF, :] = part
    along = masked[...].astype(f32) * 1000.0 / ratio[0].astype(f32)
    line = lax.broadcasted_iota(jnp.int32, (tok, tok), 0)
    lane = lax.broadcasted_iota(jnp.int32, (tok, tok), 1)
    weight = jnp.sum(jnp.where(line == lane, along, 0.0), axis=1, keepdims=True)
    copies[3].wait()
    for k in range(4):
        x = (lax.axis_index("x") + k) & 3
        for j in range(8):
            slot = x * 4 + ((lax.axis_index("zh") + j // 2) & 3)
            head = meta[PERM_AT + slot * 2 + j % 2]
            at = pl.multiple_of(head * HEAD, HEAD)
            piece = cot[:, pl.ds(at, HEAD)].astype(f32) * weight
            cols_out[k][:, j * HEAD : (j + 1) * HEAD] = piece.astype(bf16)


def piece(near, opposite, i, j):
    return (opposite[j // 2], j % 2) if i == 2 else (near[i], j)


def operands(refs, pairs, rows, at):
    r0, r1, r3, r2a, r2b, g0, g1, g3, g2a, g2b = refs
    left, right = [], []
    for dx, dy in pairs:
        ref, i = piece({0: r0, 1: r1, 3: r3}, (r2a, r2b), dx, dy)
        left.append(ref[i, rows[0] : rows[1], :])
        ref, i = piece({0: g0, 1: g1, 3: g3}, (g2a, g2b), dy, dx)
        right.append(ref[i, :, at : at + SLOT])
    return jnp.concatenate(left, axis=1), jnp.concatenate(right, axis=0)


def multiply_near(r0, r1, r3, g0, g1, g3, out):
    refs = (r0, r1, r3, None, None, g0, g1, g3, None, None)
    pairs = [(dx, dy) for dx in (0, 1, 3) for dy in (0, 1, 3)]
    for n in range(BLOCK // SLOT):
        left, right = operands(refs, pairs, (0, BLOCK), n * SLOT)
        out[:, n * SLOT : (n + 1) * SLOT] = jnp.dot(left, right, preferred_element_type=f32)


def multiply_rest(odd, near, *refs):
    refs, outs = refs[:10], refs[10:]
    z0 = lax.axis_index("z0")
    half = BLOCK // 2
    rows = (odd * half, (odd + 1) * half)
    pairs = [(dx, dy) for dx in range(4) for dy in range(4) if dx == 2 or dy == 2]
    for n in range(BLOCK // SLOT):
        left, right = operands(refs, pairs, rows, n * SLOT)
        total = near[rows[0] : rows[1], n * SLOT : (n + 1) * SLOT]
        total = (total + jnp.dot(left, right, preferred_element_type=f32)).astype(bf16)
        for out, part in zip(outs, (total[: half // 2], total[half // 2 :])):
            if odd:
                out[(n - z0) & 3] = part[:128]
                out[4 + ((n + 1 - z0) & 3)] = part[128:]
            else:
                out[2 * n] = part[:128]
                out[2 * n + 1] = part[128:]


def add_odd(mine, other, up, down):
    for j in range(4):
        up[j] = (mine[j].astype(f32) + other[j].astype(f32)).astype(bf16)
        down[j] = (mine[4 + j].astype(f32) + other[4 + j].astype(f32)).astype(bf16)


def add_even(mine, other, up, down, *outs):
    for a, out in enumerate(outs):
        for h, ref in enumerate((up, down)):
            total = mine[2 * a + h].astype(f32) + other[2 * a + h].astype(f32) + ref[a].astype(f32)
            out[h * 128 : (h + 1) * 128, :] = total.astype(out.dtype)


def gram_part(t0, t1, t2, t3, head_grad, keep, send):
    total = (t0[...] + t1[...].astype(f32)) + (t2[...].astype(f32) + t3[...].astype(f32))
    part = total.astype(bf16)
    head_grad[...] = part
    gram = lax.dot_general(part, part, (((0,), (0,)), ((), ())), preferred_element_type=f32)
    first = jnp.concatenate([gram[:HEAD, :HEAD], gram[:HALF, HEAD:]], axis=0)
    second = jnp.concatenate([gram[HEAD:, HEAD:], gram[HALF:HEAD, HEAD:]], axis=0)
    core = lax.axis_index("core")
    keep[...] = jnp.where(core == 0, first, second)
    send[...] = jnp.where(core == 0, second, first)


def product(a, b):
    return jnp.dot(a, b, precision=lax.Precision.HIGHEST, preferred_element_type=f32)


def two_terms(a):
    top = a.astype(bf16)
    return top, (a - top.astype(f32)).astype(bf16)


def short_product(a, b):
    dot = functools.partial(jnp.dot, preferred_element_type=f32)
    return (dot(a[1], b[0]) + dot(a[0], b[1])) + dot(a[0], b[0])


def newton(meta, mine, other, head_grad, o0, o1, o2, o3, result):
    core = lax.axis_index("core")
    a, b = mine[...], other[...]
    first, second = jnp.where(core == 0, a, b), jnp.where(core == 0, b, a)
    corner = jnp.concatenate([first[HEAD:], second[HEAD:]], axis=0)
    gram = jnp.concatenate(
        [
            jnp.concatenate([first[:HEAD], corner], axis=1),
            jnp.concatenate([corner.T, second[:HEAD]], axis=1),
        ],
        axis=0,
    )
    zh = lax.axis_index("zh")
    pair = lax.axis_index("x") * 4 + zh < meta[PAIRS_AT]
    row = lax.broadcasted_iota(jnp.int32, (SLOT, SLOT), 0)
    col = lax.broadcasted_iota(jnp.int32, (SLOT, SLOT), 1)
    together = jnp.logical_or((row < HEAD) == (col < HEAD), pair)
    gram = jnp.where(together, gram, 0.0)
    on_diagonal = jnp.where(row == col, gram, 0.0)
    down = jnp.sum(on_diagonal, axis=0, keepdims=True)
    across = jnp.sum(on_diagonal, axis=1, keepdims=True)
    lane, line = col[:1, :], row[:, :1]

    def factor(squares, at, axis):
        low = jnp.sum(jnp.where(at < HEAD, squares, 0.0), axis=axis, keepdims=True)
        high = jnp.sum(jnp.where(at < HEAD, 0.0, squares), axis=axis, keepdims=True)
        norm = jnp.where(pair, low + high, jnp.where(at < HEAD, low, high))
        return 1.0 / (jnp.sqrt(norm) + epsilon)

    by_col = factor(down, lane, 1)
    by_row = factor(across, line, 0)
    gram = gram * by_row * by_col
    unit = jnp.where(row == col, 1.0, 0.0)
    factors = None
    for turn in range(NS_ITERS):
        multiplied = product if turn < 2 else lambda p, q: short_product(two_terms(p), two_terms(q))
        step = quintic_a * unit + quintic_b * gram + quintic_c * multiplied(gram, gram)
        if turn < NS_ITERS - 1:
            gram = multiplied(multiplied(gram, step), step)
        factors = step if factors is None else product(factors, step)
    top, middle = two_terms(factors)
    bottom = (factors - top.astype(f32) - middle.astype(f32)).astype(bf16)
    h = head_grad[...]
    update = jnp.dot(h, bottom, preferred_element_type=f32) + jnp.dot(h, middle, preferred_element_type=f32)
    update = update + jnp.dot(h, top, preferred_element_type=f32)
    result[...] = (update * (by_col * 64.0)).astype(bf16)
    for k, out in enumerate((o0, o1, o2, o3)):
        at = pl.multiple_of(((zh + k) & 3) * HALF, HALF)
        out[...] = result[pl.ds(at, HALF), :]


def place_heads(meta, p0, p1, p2, p3, q0, q1, q2, q3, out, rows, sems):
    ylo, x, zh = lax.axis_index("ylo"), lax.axis_index("x"), lax.axis_index("zh")
    copies = []
    for i, refs in enumerate(((p0, p1, p2, p3), (q0, q1, q2, q3))):
        for dx in range(4):
            for dzh in range(4):
                slot = ((x - dx) & 3) * 4 + ((zh - dzh) & 3)
                for j in range(2):
                    at = pl.multiple_of(meta[PERM_AT + slot * 2 + j] * HEAD, HEAD)
                    rows[i, :, pl.ds(at, HEAD)] = refs[dx][dzh, :, j * HEAD : (j + 1) * HEAD].astype(f32)
        half = pl.ds(pl.multiple_of((ylo ^ i) * HALF, HALF), HALF)
        copies.append(pltpu.make_async_copy(rows.at[i], out.at[half, :], sems.at[i]))
        copies[i].start()
    for copy in copies:
        copy.wait()


Y_INDEX = (0, 2, 1, 3)


def move_x(a, k):
    return lax.ppermute(a, "x", [(i, (i + k) % 4) for i in range(4)])


def move_y(a, k):
    return lax.ppermute(a, ("ylo", "yhi"), [(Y_INDEX[i], Y_INDEX[(i + k) % 4]) for i in range(4)])


def move_z(a, k):
    return lax.ppermute(a, ("zh", "z0"), [(i, (i + k) % 8) for i in range(8)])


def swap(a, axis):
    return lax.ppermute(a, axis, [(0, 1), (1, 0)])


def farthest_first(arrays, move):
    opposite = move(arrays[2], 2)
    return [arrays[0], move(arrays[1], 1), opposite, move(arrays[3], 3)]


def on_device(activations, cotangent, masked, ratios, owners):
    tok, width = activations.shape
    *blocks, meta = local_kernel(
        prepare,
        [shape((BLOCK, tok), bf16)] * 4 + [shape((tok, BLOCK), bf16)] * 4 + [shape((PERM_AT + HEADS,), jnp.int32)],
        (owners, ratios, masked[None, :], activations, cotangent),
        16,
        2 * tok * width,
        "prepare",
        in_specs=[hbm(), hbm(), vmem(), hbm(), hbm()],
        out_specs=[vmem()] * 8 + [smem()],
        scratch=[
            pltpu.VMEM((tok, width), bf16),
            pltpu.VMEM((tok, width), bf16),
            pltpu.SMEM((HEADS,), jnp.int32),
            pltpu.SMEM((1,), jnp.int32),
            pltpu.SMEM((HEADS,), jnp.int32),
            pltpu.SMEM((HEADS,), jnp.int32),
            pltpu.SemaphoreType.DMA((4,)),
        ],
    )
    rows, cols = blocks[:4], blocks[4:]
    r0, g0 = farthest_first(rows, move_y), farthest_first(cols, move_x)
    r0, g0 = jnp.stack(r0), jnp.stack(g0)
    r1, r3 = move_x(r0, 1), move_x(r0, -1)
    g1, g3 = move_y(g0, 1), move_y(g0, -1)
    r2a, r2b = move_x(r1[:2], 1), move_x(r3[2:], -1)
    g2a, g2b = move_y(g1[:2], 1), move_y(g3[2:], -1)
    gathered = (r0, r1, r3, r2a, r2b, g0, g1, g3, g2a, g2b)

    flops = 2 * BLOCK * BLOCK * tok
    (near,) = local_kernel(
        multiply_near, [shape((BLOCK, BLOCK), f32)], (r0, r1, r3, g0, g1, g3), 32, 9 * flops, "multiply_near"
    )

    def rest(odd, name):
        return local_kernel(
            functools.partial(multiply_rest, odd),
            [shape((8, 128, SLOT), bf16)] * 2,
            (near, *gathered),
            32,
            7 * flops // 2,
            name,
        )

    own_odd, odd = rest(1, "multiply_odd")
    odd = swap(odd, "core")
    own_even, even = rest(0, "multiply_even")
    even = swap(even, "core")
    half_chunks = shape((4, 128, SLOT), bf16)
    up, down = local_kernel(
        add_odd, [half_chunks] * 2, (own_odd, odd), 8, 8 * 128 * SLOT, "add_odd"
    )
    up, down = move_z(up, 1), move_z(down, -1)
    t0, t1, t2, t3 = local_kernel(
        add_even,
        [shape((256, SLOT), f32)] + [shape((256, SLOT), bf16)] * 3,
        (own_even, even, up, down),
        8,
        16 * 128 * SLOT,
        "add_even",
    )
    t2 = move_z(t2, 4)
    t1, t3 = move_z(t1, 2), move_z(t3, 6)
    head_grad, mine, theirs = local_kernel(
        gram_part,
        [shape((256, SLOT), bf16), shape((GRAM, HEAD), f32), shape((GRAM, HEAD), f32)],
        (t0, t1, t2, t3),
        8,
        2 * 256 * SLOT * SLOT,
        "gram_part",
    )
    mine = mine + swap(theirs, "core")
    mine = mine + swap(mine, "z0")
    mine = (mine + move_y(mine, 2)) + (move_y(mine, 1) + move_y(mine, 3))
    update = local_kernel(
        newton,
        [shape((HALF, SLOT), bf16)] * 4,
        (meta, mine, swap(mine, "core"), head_grad),
        16,
        20 * 2 * SLOT**3 * 6,
        "newton",
        in_specs=[smem()] + [vmem()] * 3,
        scratch=[pltpu.VMEM((256, SLOT), bf16)],
    )
    ring = lambda a, k: lax.ppermute(a, "zh", [(i, (i + k) % 4) for i in range(4)])
    p0 = jnp.stack(farthest_first(update, ring))
    q0 = swap(p0, "ylo")
    ps, qs = farthest_first([p0] * 4, move_x), farthest_first([q0] * 4, move_x)
    (out,) = local_kernel(
        place_heads,
        [shape((2 * HALF, width), f32)],
        (meta, *ps, *qs),
        12,
        0,
        "place_heads",
        in_specs=[smem()] + [vmem()] * 8,
        out_specs=[hbm()],
        scratch=[pltpu.VMEM((2, HALF, width), f32), pltpu.SemaphoreType.DMA((2,))],
    )
    return out


def solution(mesh):
    axes = ("x", "ylo", "yhi", "zh", "z0", "core")
    fine = Mesh(mesh.devices.reshape(4, 2, 2, 4, 2, 2), axes)
    everywhere = P(axes)
    placed = (P(axes, None), P(axes, None), everywhere, everywhere, P())
    return jax.shard_map(
        on_device,
        mesh=fine,
        in_specs=placed,
        out_specs=P(("yhi", "zh", "z0", "core"), None),
        check_vma=False,
    )
```

```python
import functools

import jax
import jax.numpy as jnp
from jax import lax
from jax.experimental import pallas as pl
from jax.experimental.pallas import tpu as pltpu
from jax.sharding import Mesh
from jax.sharding import PartitionSpec as P

HEADS = 32
NS_ITERS = 5
quintic_a = 3.4445
quintic_b = -4.775
quintic_c = 2.0315
epsilon = 1e-07

PAIRS_AT, PERM_AT = 0, 8

HEAD = 128
SLOT = 2 * HEAD
BLOCK = 1024
HALF = 64
GRAM = HEAD + HALF

f32, bf16 = jnp.float32, jnp.bfloat16


def smem():
    return pl.BlockSpec(memory_space=pltpu.SMEM)


def vmem():
    return pl.BlockSpec(memory_space=pltpu.VMEM)


def hbm():
    return pl.BlockSpec(memory_space=pltpu.HBM)


def local_kernel(body, outs, operands, mib, flops, name, in_specs=None, out_specs=None, scratch=()):
    moved = sum(o.size * o.dtype.itemsize for o in list(outs) + list(operands))
    return pl.pallas_call(
        body,
        out_shape=outs,
        in_specs=in_specs or [vmem()] * len(operands),
        out_specs=out_specs or [vmem()] * len(outs),
        scratch_shapes=list(scratch),
        compiler_params=pltpu.CompilerParams(vmem_limit_bytes=mib * 2**20),
        cost_estimate=pl.CostEstimate(flops=flops, bytes_accessed=moved, transcendentals=0),
        name=name,
    )(*operands)


def shape(dims, dtype):
    return jax.ShapeDtypeStruct(dims, dtype)


def y_place():
    return lax.axis_index("yhi") * 2 + lax.axis_index("ylo")


def prepare(owners_far, ratio_far, masked, act_far, cot_far, *refs):
    rows_out, cols_out, meta = refs[:4], refs[4:8], refs[8]
    act, cot, owners, ratio, count, taken, sems = refs[9:]
    copies = [
        pltpu.make_async_copy(far, near, sems.at[i])
        for i, (far, near) in enumerate(
            ((owners_far, owners), (ratio_far, ratio), (act_far, act), (cot_far, cot))
        )
    ]
    for copy in copies:
        copy.start()
    for v in range(HEADS):
        count[v] = 0
        taken[v] = 0
    copies[0].wait()

    for h in range(HEADS):
        count[owners[h]] = count[owners[h]] + 1
    in_pairs = jnp.int32(0)
    for v in range(HEADS):
        in_pairs = in_pairs + jnp.where(count[v] > 1, 2, 0)
    next_pair, next_alone = jnp.int32(0), in_pairs
    for i in range(PERM_AT):
        meta[i] = in_pairs // 2
    for h in range(HEADS):
        owner = owners[h]
        paired = count[owner] > 1
        seen = taken[owner]
        opens = jnp.logical_and(paired, seen == 0)
        place = jnp.where(paired, jnp.where(seen == 0, next_pair, seen), next_alone)
        taken[owner] = place + 1
        meta[PERM_AT + place] = h
        next_pair = next_pair + jnp.where(opens, 2, 0)
        next_alone = next_alone + jnp.where(paired, 0, 1)

    tok, width = act.shape
    here_y, z0, core = y_place(), lax.axis_index("z0"), lax.axis_index("core")
    copies[1].wait()
    copies[2].wait()
    for k in range(4):
        y = (here_y + k) & 3
        base = (y >> 1) * (width // 2)
        low = (y & 1) * HALF
        for zrel in range(2):
            for crel in range(2):
                for zh in range(4):
                    block = zh * 4 + (z0 ^ zrel) * 2 + (core ^ crel)
                    at = pl.multiple_of(base + block * 128, 128)
                    turned = act[:, pl.ds(at, 128)].T
                    part = jnp.where(low == 0, turned[:HALF], turned[HALF:])
                    to = ((zrel * 2 + crel) * 4 + zh) * HALF
                    rows_out[k][to : to + HALF, :] = part
    along = masked[...].astype(f32) * 1000.0 / ratio[0].astype(f32)
    line = lax.broadcasted_iota(jnp.int32, (tok, tok), 0)
    lane = lax.broadcasted_iota(jnp.int32, (tok, tok), 1)
    weight = jnp.sum(jnp.where(line == lane, along, 0.0), axis=1, keepdims=True)
    copies[3].wait()
    for k in range(4):
        x = (lax.axis_index("x") + k) & 3
        for j in range(8):
            slot = x * 4 + ((lax.axis_index("zh") + j // 2) & 3)
            head = meta[PERM_AT + slot * 2 + j % 2]
            at = pl.multiple_of(head * HEAD, HEAD)
            piece = cot[:, pl.ds(at, HEAD)].astype(f32) * weight
            cols_out[k][:, j * HEAD : (j + 1) * HEAD] = piece.astype(bf16)


def piece(near, opposite, i, j):
    return (opposite[j // 2], j % 2) if i == 2 else (near[i], j)


def operands(refs, pairs, rows, at):
    r0, r1, r3, r2a, r2b, g0, g1, g3, g2a, g2b = refs
    left, right = [], []
    for dx, dy in pairs:
        ref, i = piece({0: r0, 1: r1, 3: r3}, (r2a, r2b), dx, dy)
        left.append(ref[i, rows[0] : rows[1], :])
        ref, i = piece({0: g0, 1: g1, 3: g3}, (g2a, g2b), dy, dx)
        right.append(ref[i, :, at : at + SLOT])
    return jnp.concatenate(left, axis=1), jnp.concatenate(right, axis=0)


def multiply_near(r0, r1, r3, g0, g1, g3, out):
    refs = (r0, r1, r3, None, None, g0, g1, g3, None, None)
    pairs = [(dx, dy) for dx in (0, 1, 3) for dy in (0, 1, 3)]
    for n in range(BLOCK // SLOT):
        left, right = operands(refs, pairs, (0, BLOCK), n * SLOT)
        out[:, n * SLOT : (n + 1) * SLOT] = jnp.dot(left, right, preferred_element_type=f32)


def multiply_rest(odd, near, *refs):
    refs, outs = refs[:10], refs[10:]
    z0 = lax.axis_index("z0")
    half = BLOCK // 2
    rows = (odd * half, (odd + 1) * half)
    pairs = [(dx, dy) for dx in range(4) for dy in range(4) if dx == 2 or dy == 2]
    for n in range(BLOCK // SLOT):
        left, right = operands(refs, pairs, rows, n * SLOT)
        total = near[rows[0] : rows[1], n * SLOT : (n + 1) * SLOT]
        total = (total + jnp.dot(left, right, preferred_element_type=f32)).astype(bf16)
        for out, part in zip(outs, (total[: half // 2], total[half // 2 :])):
            if odd:
                out[(n - z0) & 3] = part[:128]
                out[4 + ((n + 1 - z0) & 3)] = part[128:]
            else:
                out[2 * n] = part[:128]
                out[2 * n + 1] = part[128:]


def add_odd(mine, other, up, down):
    for j in range(4):
        up[j] = (mine[j].astype(f32) + other[j].astype(f32)).astype(bf16)
        down[j] = (mine[4 + j].astype(f32) + other[4 + j].astype(f32)).astype(bf16)


def add_even(mine, other, up, down, *outs):
    for a, out in enumerate(outs):
        for h, ref in enumerate((up, down)):
            total = mine[2 * a + h].astype(f32) + other[2 * a + h].astype(f32) + ref[a].astype(f32)
            out[h * 128 : (h + 1) * 128, :] = total.astype(out.dtype)


def gram_part(t2, t1, t3, t0, head_grad, keep, send):
    total = (t0[...] + t1[...].astype(f32)) + (t2[...].astype(f32) + t3[...].astype(f32))
    part = total.astype(bf16)
    head_grad[...] = part
    gram = lax.dot_general(part, part, (((0,), (0,)), ((), ())), preferred_element_type=f32)
    first = jnp.concatenate([gram[:HEAD, :HEAD], gram[:HALF, HEAD:]], axis=0)
    second = jnp.concatenate([gram[HEAD:, HEAD:], gram[HALF:HEAD, HEAD:]], axis=0)
    core = lax.axis_index("core")
    keep[...] = jnp.where(core == 0, first, second)
    send[...] = jnp.where(core == 0, second, first)


def product(a, b):
    return jnp.dot(a, b, precision=lax.Precision.HIGHEST, preferred_element_type=f32)


def two_terms(a):
    top = a.astype(bf16)
    return top, (a - top.astype(f32)).astype(bf16)


def short_product(a, b):
    dot = functools.partial(jnp.dot, preferred_element_type=f32)
    return (dot(a[1], b[0]) + dot(a[0], b[1])) + dot(a[0], b[0])


def newton(meta, mine, other, head_grad, out):
    core = lax.axis_index("core")
    a, b = mine[...], other[...]
    first, second = jnp.where(core == 0, a, b), jnp.where(core == 0, b, a)
    corner = jnp.concatenate([first[HEAD:], second[HEAD:]], axis=0)
    gram = jnp.concatenate(
        [
            jnp.concatenate([first[:HEAD], corner], axis=1),
            jnp.concatenate([corner.T, second[:HEAD]], axis=1),
        ],
        axis=0,
    )
    zh = lax.axis_index("zh")
    pair = lax.axis_index("x") * 4 + zh < meta[PAIRS_AT]
    row = lax.broadcasted_iota(jnp.int32, (SLOT, SLOT), 0)
    col = lax.broadcasted_iota(jnp.int32, (SLOT, SLOT), 1)
    together = jnp.logical_or((row < HEAD) == (col < HEAD), pair)
    gram = jnp.where(together, gram, 0.0)
    on_diagonal = jnp.where(row == col, gram, 0.0)
    down = jnp.sum(on_diagonal, axis=0, keepdims=True)
    across = jnp.sum(on_diagonal, axis=1, keepdims=True)
    lane, line = col[:1, :], row[:, :1]

    def factor(squares, at, axis):
        low = jnp.sum(jnp.where(at < HEAD, squares, 0.0), axis=axis, keepdims=True)
        high = jnp.sum(jnp.where(at < HEAD, 0.0, squares), axis=axis, keepdims=True)
        norm = jnp.where(pair, low + high, jnp.where(at < HEAD, low, high))
        return 1.0 / (jnp.sqrt(norm) + epsilon)

    by_col = factor(down, lane, 1)
    by_row = factor(across, line, 0)
    gram = gram * by_row * by_col
    unit = jnp.where(row == col, 1.0, 0.0)
    factors = None
    for turn in range(NS_ITERS):
        multiplied = product if turn < 2 else lambda p, q: short_product(two_terms(p), two_terms(q))
        step = quintic_a * unit + quintic_b * gram + quintic_c * multiplied(gram, gram)
        if turn < NS_ITERS - 1:
            gram = multiplied(multiplied(gram, step), step)
        factors = step if factors is None else product(factors, step)
    top, middle = two_terms(factors)
    bottom = (factors - top.astype(f32) - middle.astype(f32)).astype(bf16)
    h = head_grad[...]
    update = jnp.dot(h, bottom, preferred_element_type=f32) + jnp.dot(h, middle, preferred_element_type=f32)
    update = update + jnp.dot(h, top, preferred_element_type=f32)
    update = (update * (by_col * 64.0)).astype(bf16)
    for to in range(32):
        rows = to % 4 * HALF
        out[to] = update[rows : rows + HALF]


def place_heads(meta, update, out, rows, sems):
    copies = []
    for low in range(2):
        for slot in range(16):
            for j in range(2):
                at = pl.multiple_of(meta[PERM_AT + slot * 2 + j] * HEAD, HEAD)
                block = update[(slot // 4 * 2 + low) * 4 + slot % 4, :, j * HEAD : (j + 1) * HEAD]
                rows[low, :, pl.ds(at, HEAD)] = block.astype(f32)
        copies.append(pltpu.make_async_copy(rows.at[low], out.at[pl.ds(low * HALF, HALF), :], sems.at[low]))
        copies[low].start()
    for copy in copies:
        copy.wait()


Y_INDEX = (0, 2, 1, 3)


def move_x(a, k):
    return lax.ppermute(a, "x", [(i, (i + k) % 4) for i in range(4)])


def move_y(a, k):
    return lax.ppermute(a, ("ylo", "yhi"), [(Y_INDEX[i], Y_INDEX[(i + k) % 4]) for i in range(4)])


def move_z(a, k):
    return lax.ppermute(a, ("zh", "z0"), [(i, (i + k) % 8) for i in range(8)])


def swap(a, axis):
    return lax.ppermute(a, axis, [(0, 1), (1, 0)])


def farthest_first(arrays, move):
    opposite = move(arrays[2], 2)
    return [arrays[0], move(arrays[1], 1), opposite, move(arrays[3], 3)]


def on_device(activations, cotangent, masked, ratios, owners):
    tok, width = activations.shape
    *blocks, meta = local_kernel(
        prepare,
        [shape((BLOCK, tok), bf16)] * 4 + [shape((tok, BLOCK), bf16)] * 4 + [shape((PERM_AT + HEADS,), jnp.int32)],
        (owners, ratios, masked[None, :], activations, cotangent),
        16,
        2 * tok * width,
        "prepare",
        in_specs=[hbm(), hbm(), vmem(), hbm(), hbm()],
        out_specs=[vmem()] * 8 + [smem()],
        scratch=[
            pltpu.VMEM((tok, width), bf16),
            pltpu.VMEM((tok, width), bf16),
            pltpu.SMEM((HEADS,), jnp.int32),
            pltpu.SMEM((1,), jnp.int32),
            pltpu.SMEM((HEADS,), jnp.int32),
            pltpu.SMEM((HEADS,), jnp.int32),
            pltpu.SemaphoreType.DMA((4,)),
        ],
    )
    rows, cols = blocks[:4], blocks[4:]
    r0, g0 = farthest_first(rows, move_y), farthest_first(cols, move_x)
    r0, g0 = jnp.stack(r0), jnp.stack(g0)
    r1, r3 = move_x(r0, 1), move_x(r0, -1)
    g1, g3 = move_y(g0, 1), move_y(g0, -1)
    r2a, r2b = move_x(r1[:2], 1), move_x(r3[2:], -1)
    g2a, g2b = move_y(g1[:2], 1), move_y(g3[2:], -1)
    gathered = (r0, r1, r3, r2a, r2b, g0, g1, g3, g2a, g2b)

    flops = 2 * BLOCK * BLOCK * tok
    (near,) = local_kernel(
        multiply_near, [shape((BLOCK, BLOCK), f32)], (r0, r1, r3, g0, g1, g3), 32, 9 * flops, "multiply_near"
    )

    def rest(odd, name):
        return local_kernel(
            functools.partial(multiply_rest, odd),
            [shape((8, 128, SLOT), bf16)] * 2,
            (near, *gathered),
            32,
            7 * flops // 2,
            name,
        )

    own_odd, odd = rest(1, "multiply_odd")
    odd = swap(odd, "core")
    own_even, even = rest(0, "multiply_even")
    even = swap(even, "core")
    half_chunks = shape((4, 128, SLOT), bf16)
    up, down = local_kernel(
        add_odd, [half_chunks] * 2, (own_odd, odd), 8, 8 * 128 * SLOT, "add_odd"
    )
    up, down = move_z(up, 1), move_z(down, -1)
    t0, t1, t2, t3 = local_kernel(
        add_even,
        [shape((256, SLOT), f32)] + [shape((256, SLOT), bf16)] * 3,
        (own_even, even, up, down),
        8,
        16 * 128 * SLOT,
        "add_even",
    )
    t2 = move_z(t2, 4)
    t1, t3 = move_z(t1, 2), move_z(t3, 6)
    head_grad, mine, theirs = local_kernel(
        gram_part,
        [shape((256, SLOT), bf16), shape((GRAM, HEAD), f32), shape((GRAM, HEAD), f32)],
        (t2, t1, t3, t0),
        8,
        2 * 256 * SLOT * SLOT,
        "gram_part",
    )
    mine = mine + swap(theirs, "core")
    mine = mine + swap(mine, "z0")
    mine = (mine + move_y(mine, 2)) + (move_y(mine, 1) + move_y(mine, 3))
    (update,) = local_kernel(
        newton,
        [shape((32, HALF, SLOT), bf16)],
        (meta, mine, swap(mine, "core"), head_grad),
        16,
        20 * 2 * SLOT**3 * 6,
        "newton",
        in_specs=[smem()] + [vmem()] * 3,
    )
    update = lax.all_to_all(update, ("x", "ylo", "zh"), split_axis=0, concat_axis=0, tiled=True)
    (out,) = local_kernel(
        place_heads,
        [shape((2 * HALF, width), f32)],
        (meta, update),
        12,
        0,
        "place_heads",
        in_specs=[smem(), vmem()],
        out_specs=[hbm()],
        scratch=[pltpu.VMEM((2, HALF, width), f32), pltpu.SemaphoreType.DMA((2,))],
    )
    return out


def solution(mesh):
    axes = ("x", "ylo", "yhi", "zh", "z0", "core")
    fine = Mesh(mesh.devices.reshape(4, 2, 2, 4, 2, 2), axes)
    everywhere = P(axes)
    placed = (P(axes, None), P(axes, None), everywhere, everywhere, P())
    return jax.shard_map(
        on_device,
        mesh=fine,
        in_specs=placed,
        out_specs=P(("yhi", "zh", "z0", "core"), None),
        check_vma=False,
    )
```

```python
import functools

import jax
import jax.numpy as jnp
from jax import lax
from jax.experimental import pallas as pl
from jax.experimental.pallas import tpu as pltpu
from jax.sharding import Mesh
from jax.sharding import PartitionSpec as P

HEADS = 32
NS_ITERS = 5
quintic_a = 3.4445
quintic_b = -4.775
quintic_c = 2.0315
epsilon = 1e-07

PAIRS_AT, PERM_AT = 0, 8

HEAD = 128
SLOT = 2 * HEAD
BLOCK = 1024
HALF = 64
GRAM = HEAD + HALF

f32, bf16 = jnp.float32, jnp.bfloat16


def smem():
    return pl.BlockSpec(memory_space=pltpu.SMEM)


def vmem():
    return pl.BlockSpec(memory_space=pltpu.VMEM)


def hbm():
    return pl.BlockSpec(memory_space=pltpu.HBM)


def local_kernel(body, outs, operands, mib, flops, name, in_specs=None, out_specs=None, scratch=()):
    moved = sum(o.size * o.dtype.itemsize for o in list(outs) + list(operands))
    return pl.pallas_call(
        body,
        out_shape=outs,
        in_specs=in_specs or [vmem()] * len(operands),
        out_specs=out_specs or [vmem()] * len(outs),
        scratch_shapes=list(scratch),
        compiler_params=pltpu.CompilerParams(vmem_limit_bytes=mib * 2**20),
        cost_estimate=pl.CostEstimate(flops=flops, bytes_accessed=moved, transcendentals=0),
        name=name,
    )(*operands)


def shape(dims, dtype):
    return jax.ShapeDtypeStruct(dims, dtype)


def y_place():
    return lax.axis_index("yhi") * 2 + lax.axis_index("ylo")


def prepare(owners_far, ratio_far, masked, act_far, cot_far, *refs):
    rows_out, cols_out, meta = refs[:4], refs[4:8], refs[8]
    act, cot, owners, ratio, count, taken, sems = refs[9:]
    copies = [
        pltpu.make_async_copy(far, near, sems.at[i])
        for i, (far, near) in enumerate(
            ((owners_far, owners), (ratio_far, ratio), (act_far, act), (cot_far, cot))
        )
    ]
    for copy in copies:
        copy.start()
    for v in range(HEADS):
        count[v] = 0
        taken[v] = 0
    copies[0].wait()

    for h in range(HEADS):
        count[owners[h]] = count[owners[h]] + 1
    in_pairs = jnp.int32(0)
    for v in range(HEADS):
        in_pairs = in_pairs + jnp.where(count[v] > 1, 2, 0)
    next_pair, next_alone = jnp.int32(0), in_pairs
    for i in range(PERM_AT):
        meta[i] = in_pairs // 2
    for h in range(HEADS):
        owner = owners[h]
        paired = count[owner] > 1
        seen = taken[owner]
        opens = jnp.logical_and(paired, seen == 0)
        place = jnp.where(paired, jnp.where(seen == 0, next_pair, seen), next_alone)
        taken[owner] = place + 1
        meta[PERM_AT + place] = h
        next_pair = next_pair + jnp.where(opens, 2, 0)
        next_alone = next_alone + jnp.where(paired, 0, 1)

    tok, width = act.shape
    here_y, z0, core = y_place(), lax.axis_index("z0"), lax.axis_index("core")
    copies[1].wait()
    copies[2].wait()
    for high in range(2):
        base = ((here_y >> 1) ^ high) * (width // 2)
        for zrel in range(2):
            for crel in range(2):
                for zh in range(4):
                    block = zh * 4 + (z0 ^ zrel) * 2 + (core ^ crel)
                    at = pl.multiple_of(base + block * 128, 128)
                    turned = act[:, pl.ds(at, 128)].T
                    to = ((zrel * 2 + crel) * 4 + zh) * HALF
                    for low in range(2):
                        part = jnp.where((here_y & 1) == low, turned[:HALF], turned[HALF:])
                        rows_out[high * 2 + low][to : to + HALF, :] = part
    along = masked[...].astype(f32) * 1000.0 / ratio[0].astype(f32)
    line = lax.broadcasted_iota(jnp.int32, (tok, tok), 0)
    lane = lax.broadcasted_iota(jnp.int32, (tok, tok), 1)
    weight = jnp.sum(jnp.where(line == lane, along, 0.0), axis=1, keepdims=True)
    copies[3].wait()
    for k in range(4):
        x = lax.axis_index("x") ^ k
        for j in range(8):
            slot = x * 4 + ((lax.axis_index("zh") + j // 2) & 3)
            head = meta[PERM_AT + slot * 2 + j % 2]
            at = pl.multiple_of(head * HEAD, HEAD)
            piece = cot[:, pl.ds(at, HEAD)].astype(f32) * weight
            cols_out[k][:, j * HEAD : (j + 1) * HEAD] = piece.astype(bf16)


def piece(near, opposite, i, j):
    return (opposite[j // 2], j % 2) if i == 2 else (near[i], j)


def operands(refs, pairs, rows, at):
    r0, r1, r3, r2a, r2b, g0, g1, g3, g2a, g2b = refs
    left, right = [], []
    for dx, dy in pairs:
        ref, i = piece({0: r0, 1: r1, 3: r3}, (r2a, r2b), dx, dy)
        left.append(ref[i, rows[0] : rows[1], :])
        ref, i = piece({0: g0, 1: g1, 3: g3}, (g2a, g2b), dy, dx)
        right.append(ref[i, :, at : at + SLOT])
    return jnp.concatenate(left, axis=1), jnp.concatenate(right, axis=0)


def multiply_near(g0, r0, g1, r1, g3, r3, out):
    refs = (r0, r1, r3, None, None, g0, g1, g3, None, None)
    pairs = [(dx, dy) for dx in (0, 1, 3) for dy in (0, 1, 3)]
    for n in range(BLOCK // SLOT):
        left, right = operands(refs, pairs, (0, BLOCK), n * SLOT)
        out[:, n * SLOT : (n + 1) * SLOT] = jnp.dot(left, right, preferred_element_type=f32)


def multiply_rest(odd, near, *refs):
    refs, outs = refs[:10], refs[10:]
    z0 = lax.axis_index("z0")
    half = BLOCK // 2
    rows = (odd * half, (odd + 1) * half)
    pairs = [(dx, dy) for dx in range(4) for dy in range(4) if dx == 2 or dy == 2]
    for n in range(BLOCK // SLOT):
        left, right = operands(refs, pairs, rows, n * SLOT)
        total = near[rows[0] : rows[1], n * SLOT : (n + 1) * SLOT]
        total = (total + jnp.dot(left, right, preferred_element_type=f32)).astype(bf16)
        for out, part in zip(outs, (total[: half // 2], total[half // 2 :])):
            if odd:
                out[(n - z0) & 3] = part[:128]
                out[4 + ((n + 1 - z0) & 3)] = part[128:]
            else:
                out[2 * n] = part[:128]
                out[2 * n + 1] = part[128:]


def add_odd(mine, other, up, down):
    for j in range(4):
        up[j] = (mine[j].astype(f32) + other[j].astype(f32)).astype(bf16)
        down[j] = (mine[4 + j].astype(f32) + other[4 + j].astype(f32)).astype(bf16)


def add_even(mine, other, up, down, *outs):
    for a, out in enumerate(outs):
        for h, ref in enumerate((up, down)):
            total = mine[2 * a + h].astype(f32) + other[2 * a + h].astype(f32) + ref[a].astype(f32)
            out[h * 128 : (h + 1) * 128, :] = total.astype(out.dtype)


def gram_part(t2, t1, t3, t0, head_grad, keep, send):
    total = (t0[...] + t1[...].astype(f32)) + (t2[...].astype(f32) + t3[...].astype(f32))
    part = total.astype(bf16)
    head_grad[...] = part
    gram = lax.dot_general(part, part, (((0,), (0,)), ((), ())), preferred_element_type=f32)
    first = jnp.concatenate([gram[:HEAD, :HEAD], gram[:HALF, HEAD:]], axis=0)
    second = jnp.concatenate([gram[HEAD:, HEAD:], gram[HALF:HEAD, HEAD:]], axis=0)
    core = lax.axis_index("core")
    keep[...] = jnp.where(core == 0, first, second)
    send[...] = jnp.where(core == 0, second, first)


def product(a, b):
    return jnp.dot(a, b, precision=lax.Precision.HIGHEST, preferred_element_type=f32)


def two_terms(a):
    top = a.astype(bf16)
    return top, (a - top.astype(f32)).astype(bf16)


def short_product(a, b):
    dot = functools.partial(jnp.dot, preferred_element_type=f32)
    return (dot(a[1], b[0]) + dot(a[0], b[1])) + dot(a[0], b[0])


def newton(meta, mine, other, head_grad, o0, o1, o2, o3, result):
    core = lax.axis_index("core")
    a, b = mine[...], other[...]
    first, second = jnp.where(core == 0, a, b), jnp.where(core == 0, b, a)
    corner = jnp.concatenate([first[HEAD:], second[HEAD:]], axis=0)
    gram = jnp.concatenate(
        [
            jnp.concatenate([first[:HEAD], corner], axis=1),
            jnp.concatenate([corner.T, second[:HEAD]], axis=1),
        ],
        axis=0,
    )
    zh = lax.axis_index("zh")
    pair = lax.axis_index("x") * 4 + zh < meta[PAIRS_AT]
    row = lax.broadcasted_iota(jnp.int32, (SLOT, SLOT), 0)
    col = lax.broadcasted_iota(jnp.int32, (SLOT, SLOT), 1)
    together = jnp.logical_or((row < HEAD) == (col < HEAD), pair)
    gram = jnp.where(together, gram, 0.0)
    on_diagonal = jnp.where(row == col, gram, 0.0)
    down = jnp.sum(on_diagonal, axis=0, keepdims=True)
    across = jnp.sum(on_diagonal, axis=1, keepdims=True)
    lane, line = col[:1, :], row[:, :1]

    def factor(squares, at, axis):
        low = jnp.sum(jnp.where(at < HEAD, squares, 0.0), axis=axis, keepdims=True)
        high = jnp.sum(jnp.where(at < HEAD, 0.0, squares), axis=axis, keepdims=True)
        norm = jnp.where(pair, low + high, jnp.where(at < HEAD, low, high))
        return 1.0 / (jnp.sqrt(norm) + epsilon)

    by_col = factor(down, lane, 1)
    by_row = factor(across, line, 0)
    gram = gram * by_row * by_col
    unit = jnp.where(row == col, 1.0, 0.0)
    factors = None
    for turn in range(NS_ITERS):
        multiplied = product if turn < 2 else lambda p, q: short_product(two_terms(p), two_terms(q))
        step = quintic_a * unit + quintic_b * gram + quintic_c * multiplied(gram, gram)
        if turn < NS_ITERS - 1:
            gram = multiplied(multiplied(gram, step), step)
        factors = step if factors is None else product(factors, step)
    top, middle = two_terms(factors)
    bottom = (factors - top.astype(f32) - middle.astype(f32)).astype(bf16)
    h = head_grad[...]
    update = jnp.dot(h, bottom, preferred_element_type=f32) + jnp.dot(h, middle, preferred_element_type=f32)
    update = update + jnp.dot(h, top, preferred_element_type=f32)
    result[...] = (update * (by_col * 64.0)).astype(bf16)
    for k, out in enumerate((o0, o1, o2, o3)):
        at = pl.multiple_of((zh ^ k) * HALF, HALF)
        out[...] = result[pl.ds(at, HALF), :]


def place_heads(meta, p0, p1, p2, p3, q0, q1, q2, q3, out, rows, sems):
    ylo, x, zh = lax.axis_index("ylo"), lax.axis_index("x"), lax.axis_index("zh")
    copies = []
    for i, refs in enumerate(((p0, p1, p2, p3), (q0, q1, q2, q3))):
        for dx in range(4):
            for dzh in range(4):
                slot = (x ^ dx) * 4 + (zh ^ dzh)
                for j in range(2):
                    at = pl.multiple_of(meta[PERM_AT + slot * 2 + j] * HEAD, HEAD)
                    rows[i, :, pl.ds(at, HEAD)] = refs[dx][dzh, :, j * HEAD : (j + 1) * HEAD].astype(f32)
        half = pl.ds(pl.multiple_of((ylo ^ i) * HALF, HALF), HALF)
        copies.append(pltpu.make_async_copy(rows.at[i], out.at[half, :], sems.at[i]))
        copies[i].start()
    for copy in copies:
        copy.wait()


Y_INDEX = (0, 2, 1, 3)


def move_x(a, k):
    return lax.ppermute(a, "x", [(i, i ^ (k & 3)) for i in range(4)])


def move_y(a, k):
    return lax.ppermute(a, ("ylo", "yhi"), [(Y_INDEX[i], Y_INDEX[i ^ (k & 3)]) for i in range(4)])


def move_z(a, k):
    return lax.ppermute(a, ("zh", "z0"), [(i, (i + k) % 8) for i in range(8)])


def swap(a, axis):
    return lax.ppermute(a, axis, [(0, 1), (1, 0)])


def farthest_first(arrays, move):
    opposite = move(arrays[2], 2)
    return [arrays[0], move(arrays[1], 1), opposite, move(arrays[3], 3)]


def on_device(activations, cotangent, masked, ratios, owners):
    tok, width = activations.shape
    *blocks, meta = local_kernel(
        prepare,
        [shape((BLOCK, tok), bf16)] * 4 + [shape((tok, BLOCK), bf16)] * 4 + [shape((PERM_AT + HEADS,), jnp.int32)],
        (owners, ratios, masked[None, :], activations, cotangent),
        52,
        2 * tok * width,
        "prepare",
        in_specs=[hbm(), hbm(), vmem(), hbm(), hbm()],
        out_specs=[vmem()] * 8 + [smem()],
        scratch=[
            pltpu.VMEM((tok, width), bf16),
            pltpu.VMEM((tok, width), bf16),
            pltpu.SMEM((HEADS,), jnp.int32),
            pltpu.SMEM((1,), jnp.int32),
            pltpu.SMEM((HEADS,), jnp.int32),
            pltpu.SMEM((HEADS,), jnp.int32),
            pltpu.SemaphoreType.DMA((4,)),
        ],
    )
    rows, cols = blocks[:4], blocks[4:]
    r0, g0 = farthest_first(rows, move_y), farthest_first(cols, move_x)
    r0, g0 = jnp.stack(r0), jnp.stack(g0)
    r1, r3 = move_x(r0, 1), move_x(r0, -1)
    g1, g3 = move_y(g0, 1), move_y(g0, -1)
    r2a, r2b = move_x(r1[:2], 3), move_x(r3[2:], 1)
    g2a, g2b = move_y(g1[:2], 3), move_y(g3[2:], 1)
    gathered = (r0, r1, r3, r2a, r2b, g0, g1, g3, g2a, g2b)

    flops = 2 * BLOCK * BLOCK * tok
    (near,) = local_kernel(
        multiply_near, [shape((BLOCK, BLOCK), f32)], (g0, r0, g1, r1, g3, r3), 32, 9 * flops, "multiply_near"
    )

    def rest(odd, name):
        return local_kernel(
            functools.partial(multiply_rest, odd),
            [shape((8, 128, SLOT), bf16)] * 2,
            (near, *gathered),
            32,
            7 * flops // 2,
            name,
        )

    own_odd, odd = rest(1, "multiply_odd")
    odd = swap(odd, "core")
    own_even, even = rest(0, "multiply_even")
    even = swap(even, "core")
    half_chunks = shape((4, 128, SLOT), bf16)
    up, down = local_kernel(
        add_odd, [half_chunks] * 2, (own_odd, odd), 8, 8 * 128 * SLOT, "add_odd"
    )
    up, down = move_z(up, 1), move_z(down, -1)
    t0, t1, t2, t3 = local_kernel(
        add_even,
        [shape((256, SLOT), f32)] + [shape((256, SLOT), bf16)] * 3,
        (own_even, even, up, down),
        8,
        16 * 128 * SLOT,
        "add_even",
    )
    t2 = move_z(t2, 4)
    t1, t3 = move_z(t1, 2), move_z(t3, 6)
    head_grad, mine, theirs = local_kernel(
        gram_part,
        [shape((256, SLOT), bf16), shape((GRAM, HEAD), f32), shape((GRAM, HEAD), f32)],
        (t2, t1, t3, t0),
        8,
        2 * 256 * SLOT * SLOT,
        "gram_part",
    )
    mine = mine + swap(theirs, "core")
    mine = mine + swap(mine, "z0")
    mine = (mine + move_y(mine, 2)) + (move_y(mine, 1) + move_y(mine, 3))
    update = local_kernel(
        newton,
        [shape((HALF, SLOT), bf16)] * 4,
        (meta, mine, swap(mine, "core"), head_grad),
        16,
        20 * 2 * SLOT**3 * 6,
        "newton",
        in_specs=[smem()] + [vmem()] * 3,
        scratch=[pltpu.VMEM((256, SLOT), bf16)],
    )
    ring = lambda a, k: lax.ppermute(a, "zh", [(i, i ^ (k & 3)) for i in range(4)])
    p0 = jnp.stack(farthest_first(update, ring))
    q0 = swap(p0, "ylo")
    ps, qs = farthest_first([p0] * 4, move_x), farthest_first([q0] * 4, move_x)
    (out,) = local_kernel(
        place_heads,
        [shape((2 * HALF, width), f32)],
        (meta, *ps, *qs),
        12,
        0,
        "place_heads",
        in_specs=[smem()] + [vmem()] * 8,
        out_specs=[hbm()],
        scratch=[pltpu.VMEM((2, HALF, width), f32), pltpu.SemaphoreType.DMA((2,))],
    )
    return out


def solution(mesh):
    axes = ("x", "ylo", "yhi", "zh", "z0", "core")
    fine = Mesh(mesh.devices.reshape(4, 2, 2, 4, 2, 2), axes)
    everywhere = P(axes)
    placed = (P(axes, None), P(axes, None), everywhere, everywhere, P())
    return jax.shard_map(
        on_device,
        mesh=fine,
        in_specs=placed,
        out_specs=P(("yhi", "zh", "z0", "core"), None),
        check_vma=False,
    )
```

```python
import functools

import jax
import jax.numpy as jnp
from jax import lax
from jax.experimental import pallas as pl
from jax.experimental.pallas import tpu as pltpu
from jax.sharding import Mesh
from jax.sharding import PartitionSpec as P

HEADS = 32
NS_ITERS = 5
quintic_a = 3.4445
quintic_b = -4.775
quintic_c = 2.0315
epsilon = 1e-07

PAIRS_AT, PERM_AT = 0, 8

HEAD = 128
SLOT = 2 * HEAD
BLOCK = 1024
PLACE = (1, 2, 0, 3)
HALF = 64
GRAM = HEAD + HALF

f32, bf16 = jnp.float32, jnp.bfloat16


def smem():
    return pl.BlockSpec(memory_space=pltpu.SMEM)


def vmem():
    return pl.BlockSpec(memory_space=pltpu.VMEM)


def hbm():
    return pl.BlockSpec(memory_space=pltpu.HBM)


def local_kernel(body, outs, operands, mib, flops, name, in_specs=None, out_specs=None, scratch=()):
    moved = sum(o.size * o.dtype.itemsize for o in list(outs) + list(operands))
    return pl.pallas_call(
        body,
        out_shape=outs,
        in_specs=in_specs or [vmem()] * len(operands),
        out_specs=out_specs or [vmem()] * len(outs),
        scratch_shapes=list(scratch),
        compiler_params=pltpu.CompilerParams(vmem_limit_bytes=mib * 2**20),
        cost_estimate=pl.CostEstimate(flops=flops, bytes_accessed=moved, transcendentals=0),
        name=name,
    )(*operands)


def shape(dims, dtype):
    return jax.ShapeDtypeStruct(dims, dtype)


def y_place():
    return lax.axis_index("yhi") * 2 + lax.axis_index("ylo")


def prepare(owners_far, ratio_far, masked, act_far, cot_far, *refs):
    rows_out, cols_out, meta = refs[:4], refs[4:8], refs[8]
    act, cot, owners, ratio, count, taken, sems = refs[9:]
    copies = [
        pltpu.make_async_copy(far, near, sems.at[i])
        for i, (far, near) in enumerate(
            ((owners_far, owners), (ratio_far, ratio), (act_far, act), (cot_far, cot))
        )
    ]
    for copy in copies:
        copy.start()
    for v in range(HEADS):
        count[v] = 0
        taken[v] = 0
    copies[0].wait()

    for h in range(HEADS):
        count[owners[h]] = count[owners[h]] + 1
    in_pairs = jnp.int32(0)
    for v in range(HEADS):
        in_pairs = in_pairs + jnp.where(count[v] > 1, 2, 0)
    next_pair, next_alone = jnp.int32(0), in_pairs
    for i in range(PERM_AT):
        meta[i] = in_pairs // 2
    for h in range(HEADS):
        owner = owners[h]
        paired = count[owner] > 1
        seen = taken[owner]
        opens = jnp.logical_and(paired, seen == 0)
        place = jnp.where(paired, jnp.where(seen == 0, next_pair, seen), next_alone)
        taken[owner] = place + 1
        meta[PERM_AT + place] = h
        next_pair = next_pair + jnp.where(opens, 2, 0)
        next_alone = next_alone + jnp.where(paired, 0, 1)

    tok, width = act.shape
    here_y, z0, core = y_place(), lax.axis_index("z0"), lax.axis_index("core")
    copies[1].wait()
    copies[2].wait()
    for high in range(2):
        base = ((here_y >> 1) ^ high) * (width // 2)
        for zrel in range(2):
            for crel in range(2):
                for zh in range(4):
                    block = zh * 4 + (z0 ^ zrel) * 2 + (core ^ crel)
                    at = pl.multiple_of(base + block * 128, 128)
                    turned = act[:, pl.ds(at, 128)].T
                    to = ((zrel * 2 + crel) * 4 + zh) * HALF
                    for low in range(2):
                        part = jnp.where((here_y & 1) == low, turned[:HALF], turned[HALF:])
                        rows_out[high * 2 + low][to : to + HALF, :] = part
    along = masked[...].astype(f32) * 1000.0 / ratio[0].astype(f32)
    line = lax.broadcasted_iota(jnp.int32, (tok, tok), 0)
    lane = lax.broadcasted_iota(jnp.int32, (tok, tok), 1)
    weight = jnp.sum(jnp.where(line == lane, along, 0.0), axis=1, keepdims=True)
    copies[3].wait()
    for k in range(4):
        x = lax.axis_index("x") ^ k
        for j in range(8):
            slot = x * 4 + ((lax.axis_index("zh") + j // 2) & 3)
            head = meta[PERM_AT + slot * 2 + j % 2]
            at = pl.multiple_of(head * HEAD, HEAD)
            piece = cot[:, pl.ds(at, HEAD)].astype(f32) * weight
            cols_out[k][:, j * HEAD : (j + 1) * HEAD] = piece.astype(bf16)


def piece(near, opposite, i, j):
    j = PLACE[j]
    return (opposite[j // 2], j % 2) if i == 2 else (near[i], j)


def operands(refs, pairs, rows, at):
    r0, r1, r3, r2a, r2b, g0, g1, g3, g2a, g2b = refs
    left, right = [], []
    for dx, dy in pairs:
        ref, i = piece({0: r0, 1: r1, 3: r3}, (r2a, r2b), dx, dy)
        left.append(ref[i, rows[0] : rows[1], :])
        ref, i = piece({0: g0, 1: g1, 3: g3}, (g2a, g2b), dy, dx)
        right.append(ref[i, :, at : at + SLOT])
    return jnp.concatenate(left, axis=1), jnp.concatenate(right, axis=0)


def multiply_near(g0, r0, g1, r1, g3, r3, out):
    refs = (r0, r1, r3, None, None, g0, g1, g3, None, None)
    pairs = [(dx, dy) for dx in (0, 1, 3) for dy in (0, 1, 3)]
    for n in range(BLOCK // SLOT):
        left, right = operands(refs, pairs, (0, BLOCK), n * SLOT)
        out[:, n * SLOT : (n + 1) * SLOT] = jnp.dot(left, right, preferred_element_type=f32)


def multiply_rest(odd, near, *refs):
    refs, outs = refs[:10], refs[10:]
    z0 = lax.axis_index("z0")
    half = BLOCK // 2
    rows = (odd * half, (odd + 1) * half)
    pairs = [(dx, dy) for dx in range(4) for dy in range(4) if dx == 2 or dy == 2]
    for n in range(BLOCK // SLOT):
        left, right = operands(refs, pairs, rows, n * SLOT)
        total = near[rows[0] : rows[1], n * SLOT : (n + 1) * SLOT]
        total = (total + jnp.dot(left, right, preferred_element_type=f32)).astype(bf16)
        for out, part in zip(outs, (total[: half // 2], total[half // 2 :])):
            if odd:
                out[(n - z0) & 3] = part[:128]
                out[4 + ((n + 1 - z0) & 3)] = part[128:]
            else:
                out[2 * n] = part[:128]
                out[2 * n + 1] = part[128:]


def add_odd(mine, other, up, down):
    for j in range(4):
        up[j] = (mine[j].astype(f32) + other[j].astype(f32)).astype(bf16)
        down[j] = (mine[4 + j].astype(f32) + other[4 + j].astype(f32)).astype(bf16)


def add_even(mine, other, up, down, *outs):
    for a, out in enumerate(outs):
        for h, ref in enumerate((up, down)):
            total = mine[2 * a + h].astype(f32) + other[2 * a + h].astype(f32) + ref[a].astype(f32)
            out[h * 128 : (h + 1) * 128, :] = total.astype(out.dtype)


def gram_part(t2, t1, t3, t0, head_grad, keep, send):
    total = (t0[...] + t1[...].astype(f32)) + (t2[...].astype(f32) + t3[...].astype(f32))
    part = total.astype(bf16)
    head_grad[...] = part
    gram = lax.dot_general(part, part, (((0,), (0,)), ((), ())), preferred_element_type=f32)
    first = jnp.concatenate([gram[:HEAD, :HEAD], gram[:HALF, HEAD:]], axis=0)
    second = jnp.concatenate([gram[HEAD:, HEAD:], gram[HALF:HEAD, HEAD:]], axis=0)
    core = lax.axis_index("core")
    keep[...] = jnp.where(core == 0, first, second)
    send[...] = jnp.where(core == 0, second, first)


def product(a, b):
    return jnp.dot(a, b, precision=lax.Precision.HIGHEST, preferred_element_type=f32)


def two_terms(a):
    top = a.astype(bf16)
    return top, (a - top.astype(f32)).astype(bf16)


def short_product(a, b):
    dot = functools.partial(jnp.dot, preferred_element_type=f32)
    return (dot(a[1], b[0]) + dot(a[0], b[1])) + dot(a[0], b[0])


def newton(meta, mine, other, head_grad, o0, o1, o2, o3, result):
    core = lax.axis_index("core")
    a, b = mine[...], other[...]
    first, second = jnp.where(core == 0, a, b), jnp.where(core == 0, b, a)
    corner = jnp.concatenate([first[HEAD:], second[HEAD:]], axis=0)
    gram = jnp.concatenate(
        [
            jnp.concatenate([first[:HEAD], corner], axis=1),
            jnp.concatenate([corner.T, second[:HEAD]], axis=1),
        ],
        axis=0,
    )
    zh = lax.axis_index("zh")
    pair = lax.axis_index("x") * 4 + zh < meta[PAIRS_AT]
    row = lax.broadcasted_iota(jnp.int32, (SLOT, SLOT), 0)
    col = lax.broadcasted_iota(jnp.int32, (SLOT, SLOT), 1)
    together = jnp.logical_or((row < HEAD) == (col < HEAD), pair)
    gram = jnp.where(together, gram, 0.0)
    on_diagonal = jnp.where(row == col, gram, 0.0)
    down = jnp.sum(on_diagonal, axis=0, keepdims=True)
    across = jnp.sum(on_diagonal, axis=1, keepdims=True)
    lane, line = col[:1, :], row[:, :1]

    def factor(squares, at, axis):
        low = jnp.sum(jnp.where(at < HEAD, squares, 0.0), axis=axis, keepdims=True)
        high = jnp.sum(jnp.where(at < HEAD, 0.0, squares), axis=axis, keepdims=True)
        norm = jnp.where(pair, low + high, jnp.where(at < HEAD, low, high))
        return 1.0 / (jnp.sqrt(norm) + epsilon)

    by_col = factor(down, lane, 1)
    by_row = factor(across, line, 0)
    gram = gram * by_row * by_col
    unit = jnp.where(row == col, 1.0, 0.0)
    factors = None
    for turn in range(NS_ITERS):
        multiplied = product if turn < 2 else lambda p, q: short_product(two_terms(p), two_terms(q))
        step = quintic_a * unit + quintic_b * gram + quintic_c * multiplied(gram, gram)
        if turn < NS_ITERS - 1:
            gram = multiplied(multiplied(gram, step), step)
        factors = step if factors is None else product(factors, step)
    top, middle = two_terms(factors)
    bottom = (factors - top.astype(f32) - middle.astype(f32)).astype(bf16)
    h = head_grad[...]
    update = jnp.dot(h, bottom, preferred_element_type=f32) + jnp.dot(h, middle, preferred_element_type=f32)
    update = update + jnp.dot(h, top, preferred_element_type=f32)
    result[...] = (update * (by_col * 64.0)).astype(bf16)
    for k, out in enumerate((o0, o1, o2, o3)):
        at = pl.multiple_of((zh ^ k) * HALF, HALF)
        out[...] = result[pl.ds(at, HALF), :]


def place_heads(meta, p0, p1, p2, p3, q0, q1, q2, q3, out, rows, sems):
    ylo, x, zh = lax.axis_index("ylo"), lax.axis_index("x"), lax.axis_index("zh")
    copies = []
    for i, refs in enumerate(((p0, p1, p2, p3), (q0, q1, q2, q3))):
        for dx in range(4):
            for dzh in range(4):
                slot = (x ^ dx) * 4 + (zh ^ dzh)
                for j in range(2):
                    at = pl.multiple_of(meta[PERM_AT + slot * 2 + j] * HEAD, HEAD)
                    rows[i, :, pl.ds(at, HEAD)] = refs[dx][dzh, :, j * HEAD : (j + 1) * HEAD].astype(f32)
        half = pl.ds(pl.multiple_of((ylo ^ i) * HALF, HALF), HALF)
        copies.append(pltpu.make_async_copy(rows.at[i], out.at[half, :], sems.at[i]))
        copies[i].start()
    for copy in copies:
        copy.wait()


Y_INDEX = (0, 2, 1, 3)


def move_x(a, k):
    return lax.ppermute(a, "x", [(i, i ^ (k & 3)) for i in range(4)])


def move_y(a, k):
    return lax.ppermute(a, ("ylo", "yhi"), [(Y_INDEX[i], Y_INDEX[i ^ (k & 3)]) for i in range(4)])


def move_z(a, k):
    return lax.ppermute(a, ("zh", "z0"), [(i, (i + k) % 8) for i in range(8)])


def swap(a, axis):
    return lax.ppermute(a, axis, [(0, 1), (1, 0)])


def farthest_first(arrays, move):
    opposite = move(arrays[2], 2)
    return [arrays[0], move(arrays[1], 1), opposite, move(arrays[3], 3)]


def far_to_front(arrays):
    return [arrays[2], arrays[0], arrays[1], arrays[3]]


def on_device(activations, cotangent, masked, ratios, owners):
    tok, width = activations.shape
    *blocks, meta = local_kernel(
        prepare,
        [shape((BLOCK, tok), bf16)] * 4 + [shape((tok, BLOCK), bf16)] * 4 + [shape((PERM_AT + HEADS,), jnp.int32)],
        (owners, ratios, masked[None, :], activations, cotangent),
        52,
        2 * tok * width,
        "prepare",
        in_specs=[hbm(), hbm(), vmem(), hbm(), hbm()],
        out_specs=[vmem()] * 8 + [smem()],
        scratch=[
            pltpu.VMEM((tok, width), bf16),
            pltpu.VMEM((tok, width), bf16),
            pltpu.SMEM((HEADS,), jnp.int32),
            pltpu.SMEM((1,), jnp.int32),
            pltpu.SMEM((HEADS,), jnp.int32),
            pltpu.SMEM((HEADS,), jnp.int32),
            pltpu.SemaphoreType.DMA((4,)),
        ],
    )
    rows, cols = blocks[:4], blocks[4:]
    r0, g0 = farthest_first(rows, move_y), farthest_first(cols, move_x)
    r0, g0 = jnp.stack(far_to_front(r0)), jnp.stack(far_to_front(g0))
    r1, r3 = move_x(r0, 1), move_x(r0, -1)
    g1, g3 = move_y(g0, 1), move_y(g0, -1)
    r2a, r2b = move_x(r1[:2], 3), move_x(r3[2:], 1)
    g2a, g2b = move_y(g1[:2], 3), move_y(g3[2:], 1)
    gathered = (r0, r1, r3, r2a, r2b, g0, g1, g3, g2a, g2b)

    flops = 2 * BLOCK * BLOCK * tok
    (near,) = local_kernel(
        multiply_near, [shape((BLOCK, BLOCK), f32)], (g0, r0, g1, r1, g3, r3), 32, 9 * flops, "multiply_near"
    )

    def rest(odd, name):
        return local_kernel(
            functools.partial(multiply_rest, odd),
            [shape((8, 128, SLOT), bf16)] * 2,
            (near, *gathered),
            32,
            7 * flops // 2,
            name,
        )

    own_odd, odd = rest(1, "multiply_odd")
    odd = swap(odd, "core")
    own_even, even = rest(0, "multiply_even")
    even = swap(even, "core")
    half_chunks = shape((4, 128, SLOT), bf16)
    up, down = local_kernel(
        add_odd, [half_chunks] * 2, (own_odd, odd), 8, 8 * 128 * SLOT, "add_odd"
    )
    up, down = move_z(up, 1), move_z(down, -1)
    t0, t1, t2, t3 = local_kernel(
        add_even,
        [shape((256, SLOT), f32)] + [shape((256, SLOT), bf16)] * 3,
        (own_even, even, up, down),
        8,
        16 * 128 * SLOT,
        "add_even",
    )
    t2 = move_z(t2, 4)
    t1, t3 = move_z(t1, 2), move_z(t3, 6)
    head_grad, mine, theirs = local_kernel(
        gram_part,
        [shape((256, SLOT), bf16), shape((GRAM, HEAD), f32), shape((GRAM, HEAD), f32)],
        (t2, t1, t3, t0),
        8,
        2 * 256 * SLOT * SLOT,
        "gram_part",
    )
    mine = mine + swap(theirs, "core")
    mine = mine + swap(mine, "z0")
    mine = (mine + move_y(mine, 2)) + (move_y(mine, 1) + move_y(mine, 3))
    update = local_kernel(
        newton,
        [shape((HALF, SLOT), bf16)] * 4,
        (meta, mine, swap(mine, "core"), head_grad),
        16,
        20 * 2 * SLOT**3 * 6,
        "newton",
        in_specs=[smem()] + [vmem()] * 3,
        scratch=[pltpu.VMEM((256, SLOT), bf16)],
    )
    ring = lambda a, k: lax.ppermute(a, "zh", [(i, i ^ (k & 3)) for i in range(4)])
    p0 = jnp.stack(farthest_first(update, ring))
    q0 = swap(p0, "ylo")
    ps = farthest_first([p0] * 4, move_x)
    qs = [q0, move_x(q0, 1), swap(ps[2], "ylo"), swap(ps[3], "ylo")]
    (out,) = local_kernel(
        place_heads,
        [shape((2 * HALF, width), f32)],
        (meta, *ps, *qs),
        12,
        0,
        "place_heads",
        in_specs=[smem()] + [vmem()] * 8,
        out_specs=[hbm()],
        scratch=[pltpu.VMEM((2, HALF, width), f32), pltpu.SemaphoreType.DMA((2,))],
    )
    return out


def solution(mesh):
    axes = ("x", "ylo", "yhi", "zh", "z0", "core")
    fine = Mesh(mesh.devices.reshape(4, 2, 2, 4, 2, 2), axes)
    everywhere = P(axes)
    placed = (P(axes, None), P(axes, None), everywhere, everywhere, P())
    return jax.shard_map(
        on_device,
        mesh=fine,
        in_specs=placed,
        out_specs=P(("yhi", "zh", "z0", "core"), None),
        check_vma=False,
    )
```

```python
import functools

import jax
import jax.numpy as jnp
from jax import lax
from jax.experimental import pallas as pl
from jax.experimental.pallas import tpu as pltpu
from jax.sharding import Mesh
from jax.sharding import PartitionSpec as P

HEADS = 32
NS_ITERS = 5
quintic_a = 3.4445
quintic_b = -4.775
quintic_c = 2.0315
epsilon = 1e-07

PAIRS_AT, PERM_AT = 0, 8

HEAD = 128
SLOT = 2 * HEAD
BLOCK = 1024
PLACE = (1, 2, 0, 3)
HALF = 64
GRAM = HEAD + HALF

f32, bf16 = jnp.float32, jnp.bfloat16


def smem():
    return pl.BlockSpec(memory_space=pltpu.SMEM)


def vmem():
    return pl.BlockSpec(memory_space=pltpu.VMEM)


def hbm():
    return pl.BlockSpec(memory_space=pltpu.HBM)


def local_kernel(body, outs, operands, mib, flops, name, in_specs=None, out_specs=None, scratch=(), aliases=None):
    moved = sum(o.size * o.dtype.itemsize for o in list(outs) + list(operands))
    return pl.pallas_call(
        body,
        out_shape=outs,
        in_specs=in_specs or [vmem()] * len(operands),
        out_specs=out_specs or [vmem()] * len(outs),
        scratch_shapes=list(scratch),
        input_output_aliases=aliases or {},
        compiler_params=pltpu.CompilerParams(vmem_limit_bytes=mib * 2**20),
        cost_estimate=pl.CostEstimate(flops=flops, bytes_accessed=moved, transcendentals=0),
        name=name,
    )(*operands)


def shape(dims, dtype):
    return jax.ShapeDtypeStruct(dims, dtype)


def y_place():
    return lax.axis_index("yhi") * 2 + lax.axis_index("ylo")


def prepare(owners_far, ratio_far, masked, act_far, cot_far, *refs):
    rows_out, cols_out, meta = refs[:4], refs[4:8], refs[8]
    act, cot, owners, ratio, count, taken, sems = refs[9:]
    copies = [
        pltpu.make_async_copy(far, near, sems.at[i])
        for i, (far, near) in enumerate(
            ((owners_far, owners), (ratio_far, ratio), (act_far, act), (cot_far, cot))
        )
    ]
    for copy in copies:
        copy.start()
    for v in range(HEADS):
        count[v] = 0
        taken[v] = 0
    copies[0].wait()

    for h in range(HEADS):
        count[owners[h]] = count[owners[h]] + 1
    in_pairs = jnp.int32(0)
    for v in range(HEADS):
        in_pairs = in_pairs + jnp.where(count[v] > 1, 2, 0)
    next_pair, next_alone = jnp.int32(0), in_pairs
    for i in range(PERM_AT):
        meta[i] = in_pairs // 2
    for h in range(HEADS):
        owner = owners[h]
        paired = count[owner] > 1
        seen = taken[owner]
        opens = jnp.logical_and(paired, seen == 0)
        place = jnp.where(paired, jnp.where(seen == 0, next_pair, seen), next_alone)
        taken[owner] = place + 1
        meta[PERM_AT + place] = h
        next_pair = next_pair + jnp.where(opens, 2, 0)
        next_alone = next_alone + jnp.where(paired, 0, 1)

    tok, width = act.shape
    here_y, z0, core = y_place(), lax.axis_index("z0"), lax.axis_index("core")
    copies[1].wait()
    copies[2].wait()
    for high in range(2):
        base = ((here_y >> 1) ^ high) * (width // 2)
        for zrel in range(2):
            for crel in range(2):
                for zh in range(4):
                    block = zh * 4 + (z0 ^ zrel) * 2 + (core ^ crel)
                    at = pl.multiple_of(base + block * 128, 128)
                    turned = act[:, pl.ds(at, 128)].T
                    to = ((zrel * 2 + crel) * 4 + zh) * HALF
                    for low in range(2):
                        part = jnp.where((here_y & 1) == low, turned[:HALF], turned[HALF:])
                        rows_out[high * 2 + low][to : to + HALF, :] = part
    along = masked[...].astype(f32) * 1000.0 / ratio[0].astype(f32)
    line = lax.broadcasted_iota(jnp.int32, (tok, tok), 0)
    lane = lax.broadcasted_iota(jnp.int32, (tok, tok), 1)
    weight = jnp.sum(jnp.where(line == lane, along, 0.0), axis=1, keepdims=True)
    copies[3].wait()
    for k in range(4):
        x = lax.axis_index("x") ^ k
        for j in range(8):
            slot = x * 4 + ((lax.axis_index("zh") + j // 2) & 3)
            head = meta[PERM_AT + slot * 2 + j % 2]
            at = pl.multiple_of(head * HEAD, HEAD)
            piece = cot[:, pl.ds(at, HEAD)].astype(f32) * weight
            cols_out[k][:, j * HEAD : (j + 1) * HEAD] = piece.astype(bf16)


def piece(near, opposite, i, j):
    j = PLACE[j]
    return (opposite[j // 2], j % 2) if i == 2 else (near[i], j)


def operands(refs, pairs, rows, at):
    r0, r1, r3, r2a, r2b, g0, g1, g3, g2a, g2b = refs
    left, right = [], []
    for dx, dy in pairs:
        ref, i = piece({0: r0, 1: r1, 3: r3}, (r2a, r2b), dx, dy)
        left.append(ref[i, rows[0] : rows[1], :])
        ref, i = piece({0: g0, 1: g1, 3: g3}, (g2a, g2b), dy, dx)
        right.append(ref[i, :, at : at + SLOT])
    return jnp.concatenate(left, axis=1), jnp.concatenate(right, axis=0)


def multiply_near(g0, r0, g1, r1, g3, r3, out):
    refs = (r0, r1, r3, None, None, g0, g1, g3, None, None)
    pairs = [(dx, dy) for dx in (0, 1, 3) for dy in (0, 1, 3)]
    for n in range(BLOCK // SLOT):
        left, right = operands(refs, pairs, (0, BLOCK), n * SLOT)
        out[:, n * SLOT : (n + 1) * SLOT] = jnp.dot(left, right, preferred_element_type=f32)


def multiply_rest(odd, near, *refs):
    refs, outs = refs[:10], refs[10:]
    z0 = lax.axis_index("z0")
    half = BLOCK // 2
    rows = (odd * half, (odd + 1) * half)
    pairs = [(dx, dy) for dx in range(4) for dy in range(4) if dx == 2 or dy == 2]
    for n in range(BLOCK // SLOT):
        left, right = operands(refs, pairs, rows, n * SLOT)
        total = near[rows[0] : rows[1], n * SLOT : (n + 1) * SLOT]
        total = (total + jnp.dot(left, right, preferred_element_type=f32)).astype(bf16)
        for out, part in zip(outs, (total[: half // 2], total[half // 2 :])):
            if odd:
                out[(n - z0) & 3] = part[:128]
                out[4 + ((n + 1 - z0) & 3)] = part[128:]
            else:
                out[2 * n] = part[:128]
                out[2 * n + 1] = part[128:]


def add_odd(mine, other, up, down):
    for j in range(4):
        up[j] = (mine[j].astype(f32) + other[j].astype(f32)).astype(bf16)
        down[j] = (mine[4 + j].astype(f32) + other[4 + j].astype(f32)).astype(bf16)


def add_even(mine, other, up, down, *outs):
    for a, out in enumerate(outs):
        for h, ref in enumerate((up, down)):
            total = mine[2 * a + h].astype(f32) + other[2 * a + h].astype(f32) + ref[a].astype(f32)
            out[h * 128 : (h + 1) * 128, :] = total.astype(out.dtype)


def gram_part(t2, t1, t3, t0, head_grad, keep, send):
    total = (t0[...] + t1[...].astype(f32)) + (t2[...].astype(f32) + t3[...].astype(f32))
    part = total.astype(bf16)
    head_grad[...] = part
    gram = lax.dot_general(part, part, (((0,), (0,)), ((), ())), preferred_element_type=f32)
    first = jnp.concatenate([gram[:HEAD, :HEAD], gram[:HALF, HEAD:]], axis=0)
    second = jnp.concatenate([gram[HEAD:, HEAD:], gram[HALF:HEAD, HEAD:]], axis=0)
    core = lax.axis_index("core")
    keep[...] = jnp.where(core == 0, first, second)
    send[...] = jnp.where(core == 0, second, first)


def product(a, b):
    return jnp.dot(a, b, precision=lax.Precision.HIGHEST, preferred_element_type=f32)


def two_terms(a):
    top = a.astype(bf16)
    return top, (a - top.astype(f32)).astype(bf16)


def short_product(a, b):
    dot = functools.partial(jnp.dot, preferred_element_type=f32)
    return (dot(a[1], b[0]) + dot(a[0], b[1])) + dot(a[0], b[0])


def newton(meta, mine, other, head_grad, o0, o1, o2, o3, result):
    core = lax.axis_index("core")
    a, b = mine[...], other[...]
    first, second = jnp.where(core == 0, a, b), jnp.where(core == 0, b, a)
    corner = jnp.concatenate([first[HEAD:], second[HEAD:]], axis=0)
    gram = jnp.concatenate(
        [
            jnp.concatenate([first[:HEAD], corner], axis=1),
            jnp.concatenate([corner.T, second[:HEAD]], axis=1),
        ],
        axis=0,
    )
    zh = lax.axis_index("zh")
    pair = lax.axis_index("x") * 4 + zh < meta[PAIRS_AT]
    row = lax.broadcasted_iota(jnp.int32, (SLOT, SLOT), 0)
    col = lax.broadcasted_iota(jnp.int32, (SLOT, SLOT), 1)
    together = jnp.logical_or((row < HEAD) == (col < HEAD), pair)
    gram = jnp.where(together, gram, 0.0)
    on_diagonal = jnp.where(row == col, gram, 0.0)
    down = jnp.sum(on_diagonal, axis=0, keepdims=True)
    across = jnp.sum(on_diagonal, axis=1, keepdims=True)
    lane, line = col[:1, :], row[:, :1]

    def factor(squares, at, axis):
        low = jnp.sum(jnp.where(at < HEAD, squares, 0.0), axis=axis, keepdims=True)
        high = jnp.sum(jnp.where(at < HEAD, 0.0, squares), axis=axis, keepdims=True)
        norm = jnp.where(pair, low + high, jnp.where(at < HEAD, low, high))
        return 1.0 / (jnp.sqrt(norm) + epsilon)

    by_col = factor(down, lane, 1)
    by_row = factor(across, line, 0)
    gram = gram * by_row * by_col
    unit = jnp.where(row == col, 1.0, 0.0)
    factors = None
    for turn in range(NS_ITERS):
        multiplied = product if turn < 2 else lambda p, q: short_product(two_terms(p), two_terms(q))
        step = quintic_a * unit + quintic_b * gram + quintic_c * multiplied(gram, gram)
        if turn < NS_ITERS - 1:
            gram = multiplied(multiplied(gram, step), step)
        factors = step if factors is None else product(factors, step)
    top, middle = two_terms(factors)
    bottom = (factors - top.astype(f32) - middle.astype(f32)).astype(bf16)
    h = head_grad[...]
    update = jnp.dot(h, bottom, preferred_element_type=f32) + jnp.dot(h, middle, preferred_element_type=f32)
    update = update + jnp.dot(h, top, preferred_element_type=f32)
    result[...] = (update * (by_col * 64.0)).astype(bf16)
    for k, out in enumerate((o0, o1, o2, o3)):
        at = pl.multiple_of((zh ^ k) * HALF, HALF)
        out[...] = result[pl.ds(at, HALF), :]


def place_heads(other, meta, *refs):
    blocks, (out, rows, sem) = refs[:4], refs[-3:]
    ylo, x, zh = lax.axis_index("ylo"), lax.axis_index("x"), lax.axis_index("zh")
    for dx in range(4):
        for dzh in range(4):
            slot = (x ^ dx) * 4 + (zh ^ dzh)
            for j in range(2):
                at = pl.multiple_of(meta[PERM_AT + slot * 2 + j] * HEAD, HEAD)
                rows[:, pl.ds(at, HEAD)] = blocks[dx][dzh, :, j * HEAD : (j + 1) * HEAD].astype(f32)
    half = pl.ds(pl.multiple_of((ylo ^ other) * HALF, HALF), HALF)
    copy = pltpu.make_async_copy(rows, out.at[half, :], sem)
    copy.start()
    copy.wait()


Y_INDEX = (0, 2, 1, 3)


def move_x(a, k):
    return lax.ppermute(a, "x", [(i, i ^ (k & 3)) for i in range(4)])


def move_y(a, k):
    return lax.ppermute(a, ("ylo", "yhi"), [(Y_INDEX[i], Y_INDEX[i ^ (k & 3)]) for i in range(4)])


def move_z(a, k):
    return lax.ppermute(a, ("zh", "z0"), [(i, (i + k) % 8) for i in range(8)])


def swap(a, axis):
    return lax.ppermute(a, axis, [(0, 1), (1, 0)])


def farthest_first(arrays, move):
    opposite = move(arrays[2], 2)
    return [arrays[0], move(arrays[1], 1), opposite, move(arrays[3], 3)]


def far_to_front(arrays):
    return [arrays[2], arrays[0], arrays[1], arrays[3]]


def on_device(activations, cotangent, masked, ratios, owners):
    tok, width = activations.shape
    *blocks, meta = local_kernel(
        prepare,
        [shape((BLOCK, tok), bf16)] * 4 + [shape((tok, BLOCK), bf16)] * 4 + [shape((PERM_AT + HEADS,), jnp.int32)],
        (owners, ratios, masked[None, :], activations, cotangent),
        52,
        2 * tok * width,
        "prepare",
        in_specs=[hbm(), hbm(), vmem(), hbm(), hbm()],
        out_specs=[vmem()] * 8 + [smem()],
        scratch=[
            pltpu.VMEM((tok, width), bf16),
            pltpu.VMEM((tok, width), bf16),
            pltpu.SMEM((HEADS,), jnp.int32),
            pltpu.SMEM((1,), jnp.int32),
            pltpu.SMEM((HEADS,), jnp.int32),
            pltpu.SMEM((HEADS,), jnp.int32),
            pltpu.SemaphoreType.DMA((4,)),
        ],
    )
    rows, cols = blocks[:4], blocks[4:]
    r0, g0 = farthest_first(rows, move_y), farthest_first(cols, move_x)
    r0, g0 = jnp.stack(far_to_front(r0)), jnp.stack(far_to_front(g0))
    r1, r3 = move_x(r0, 1), move_x(r0, -1)
    g1, g3 = move_y(g0, 1), move_y(g0, -1)
    r2a, r2b = move_x(r1[:2], 3), move_x(r3[2:], 1)
    g2a, g2b = move_y(g1[:2], 3), move_y(g3[2:], 1)
    gathered = (r0, r1, r3, r2a, r2b, g0, g1, g3, g2a, g2b)

    flops = 2 * BLOCK * BLOCK * tok
    (near,) = local_kernel(
        multiply_near, [shape((BLOCK, BLOCK), f32)], (g0, r0, g1, r1, g3, r3), 32, 9 * flops, "multiply_near"
    )

    def rest(odd, name):
        return local_kernel(
            functools.partial(multiply_rest, odd),
            [shape((8, 128, SLOT), bf16)] * 2,
            (near, *gathered),
            32,
            7 * flops // 2,
            name,
        )

    own_odd, odd = rest(1, "multiply_odd")
    odd = swap(odd, "core")
    own_even, even = rest(0, "multiply_even")
    even = swap(even, "core")
    half_chunks = shape((4, 128, SLOT), bf16)
    up, down = local_kernel(
        add_odd, [half_chunks] * 2, (own_odd, odd), 8, 8 * 128 * SLOT, "add_odd"
    )
    up, down = move_z(up, 1), move_z(down, -1)
    t0, t1, t2, t3 = local_kernel(
        add_even,
        [shape((256, SLOT), f32)] + [shape((256, SLOT), bf16)] * 3,
        (own_even, even, up, down),
        8,
        16 * 128 * SLOT,
        "add_even",
    )
    t2 = move_z(t2, 4)
    t1, t3 = move_z(t1, 2), move_z(t3, 6)
    head_grad, mine, theirs = local_kernel(
        gram_part,
        [shape((256, SLOT), bf16), shape((GRAM, HEAD), f32), shape((GRAM, HEAD), f32)],
        (t2, t1, t3, t0),
        8,
        2 * 256 * SLOT * SLOT,
        "gram_part",
    )
    mine = mine + swap(theirs, "core")
    mine = mine + swap(mine, "z0")
    mine = (mine + move_y(mine, 2)) + (move_y(mine, 1) + move_y(mine, 3))
    update = local_kernel(
        newton,
        [shape((HALF, SLOT), bf16)] * 4,
        (meta, mine, swap(mine, "core"), head_grad),
        16,
        20 * 2 * SLOT**3 * 6,
        "newton",
        in_specs=[smem()] + [vmem()] * 3,
        scratch=[pltpu.VMEM((256, SLOT), bf16)],
    )
    ring = lambda a, k: lax.ppermute(a, "zh", [(i, i ^ (k & 3)) for i in range(4)])
    p0 = jnp.stack(farthest_first(update, ring))
    q0 = swap(p0, "ylo")
    ps = farthest_first([p0] * 4, move_x)
    qs = [q0, move_x(q0, 1), swap(ps[2], "ylo"), swap(ps[3], "ylo")]
    out = None
    for other, blocks in enumerate((ps, qs)):
        earlier = [] if out is None else [out]
        (out,) = local_kernel(
            functools.partial(place_heads, other),
            [shape((2 * HALF, width), f32)],
            (meta, *blocks, *earlier),
            12,
            0,
            "place_other" if other else "place_own",
            in_specs=[smem()] + [vmem()] * 4 + [hbm()] * len(earlier),
            out_specs=[hbm()],
            scratch=[pltpu.VMEM((HALF, width), f32), pltpu.SemaphoreType.DMA],
            aliases={5: 0} if earlier else {},
        )
    return out


def solution(mesh):
    axes = ("x", "ylo", "yhi", "zh", "z0", "core")
    fine = Mesh(mesh.devices.reshape(4, 2, 2, 4, 2, 2), axes)
    everywhere = P(axes)
    placed = (P(axes, None), P(axes, None), everywhere, everywhere, P())
    return jax.shard_map(
        on_device,
        mesh=fine,
        in_specs=placed,
        out_specs=P(("yhi", "zh", "z0", "core"), None),
        check_vma=False,
    )
```

```python
import functools

import jax
import jax.numpy as jnp
from jax import lax
from jax.experimental import pallas as pl
from jax.experimental.pallas import tpu as pltpu
from jax.sharding import Mesh
from jax.sharding import PartitionSpec as P

HEADS = 32
NS_ITERS = 5
quintic_a = 3.4445
quintic_b = -4.775
quintic_c = 2.0315
epsilon = 1e-07

PAIRS_AT, PERM_AT = 0, 8

HEAD = 128
SLOT = 2 * HEAD
BLOCK = 1024
PLACE = (1, 2, 0, 3)
HALF = 64
GRAM = HEAD + HALF

f32, bf16 = jnp.float32, jnp.bfloat16


def smem():
    return pl.BlockSpec(memory_space=pltpu.SMEM)


def vmem():
    return pl.BlockSpec(memory_space=pltpu.VMEM)


def hbm():
    return pl.BlockSpec(memory_space=pltpu.HBM)


def local_kernel(body, outs, operands, mib, flops, name, in_specs=None, out_specs=None, scratch=(), aliases=None):
    moved = sum(o.size * o.dtype.itemsize for o in list(outs) + list(operands))
    return pl.pallas_call(
        body,
        out_shape=outs,
        in_specs=in_specs or [vmem()] * len(operands),
        out_specs=out_specs or [vmem()] * len(outs),
        scratch_shapes=list(scratch),
        input_output_aliases=aliases or {},
        compiler_params=pltpu.CompilerParams(vmem_limit_bytes=mib * 2**20),
        cost_estimate=pl.CostEstimate(flops=flops, bytes_accessed=moved, transcendentals=0),
        name=name,
    )(*operands)


def shape(dims, dtype):
    return jax.ShapeDtypeStruct(dims, dtype)


def y_place():
    return lax.axis_index("yhi") * 2 + lax.axis_index("ylo")


def prepare(owners_far, ratio_far, masked, act_far, cot_far, *refs):
    rows_out, cols_out, meta = refs[:4], refs[4:8], refs[8]
    act, cot, owners, ratio, count, taken, sems = refs[9:]
    copies = [
        pltpu.make_async_copy(far, near, sems.at[i])
        for i, (far, near) in enumerate(
            ((owners_far, owners), (ratio_far, ratio), (act_far, act), (cot_far, cot))
        )
    ]
    for copy in copies:
        copy.start()
    for v in range(HEADS):
        count[v] = 0
        taken[v] = 0
    copies[0].wait()

    for h in range(HEADS):
        count[owners[h]] = count[owners[h]] + 1
    in_pairs = jnp.int32(0)
    for v in range(HEADS):
        in_pairs = in_pairs + jnp.where(count[v] > 1, 2, 0)
    next_pair, next_alone = jnp.int32(0), in_pairs
    for i in range(PERM_AT):
        meta[i] = in_pairs // 2
    for h in range(HEADS):
        owner = owners[h]
        paired = count[owner] > 1
        seen = taken[owner]
        opens = jnp.logical_and(paired, seen == 0)
        place = jnp.where(paired, jnp.where(seen == 0, next_pair, seen), next_alone)
        taken[owner] = place + 1
        meta[PERM_AT + place] = h
        next_pair = next_pair + jnp.where(opens, 2, 0)
        next_alone = next_alone + jnp.where(paired, 0, 1)

    tok, width = act.shape
    here_y, z0, core = y_place(), lax.axis_index("z0"), lax.axis_index("core")
    copies[1].wait()
    copies[2].wait()
    for high in range(2):
        base = ((here_y >> 1) ^ high) * (width // 2)
        for zrel in range(2):
            for crel in range(2):
                for zh in range(4):
                    block = zh * 4 + (z0 ^ zrel) * 2 + (core ^ crel)
                    at = pl.multiple_of(base + block * 128, 128)
                    turned = act[:, pl.ds(at, 128)].T
                    to = ((zrel * 2 + crel) * 4 + zh) * HALF
                    for low in range(2):
                        part = jnp.where((here_y & 1) == low, turned[:HALF], turned[HALF:])
                        rows_out[high * 2 + low][to : to + HALF, :] = part
    along = masked[...].astype(f32) * 1000.0 / ratio[0].astype(f32)
    line = lax.broadcasted_iota(jnp.int32, (tok, tok), 0)
    lane = lax.broadcasted_iota(jnp.int32, (tok, tok), 1)
    weight = jnp.sum(jnp.where(line == lane, along, 0.0), axis=1, keepdims=True)
    copies[3].wait()
    for k in range(4):
        x = lax.axis_index("x") ^ k
        for j in range(8):
            slot = x * 4 + ((lax.axis_index("zh") + j // 2) & 3)
            head = meta[PERM_AT + slot * 2 + j % 2]
            at = pl.multiple_of(head * HEAD, HEAD)
            piece = cot[:, pl.ds(at, HEAD)].astype(f32) * weight
            cols_out[k][:, j * HEAD : (j + 1) * HEAD] = piece.astype(bf16)


def piece(near, opposite, i, j):
    j = PLACE[j]
    return (opposite[j // 2], j % 2) if i == 2 else (near[i], j)


def operands(refs, pairs, rows, at):
    r0, r1, r3, r2a, r2b, g0, g1, g3, g2a, g2b = refs
    left, right = [], []
    for dx, dy in pairs:
        ref, i = piece({0: r0, 1: r1, 3: r3}, (r2a, r2b), dx, dy)
        left.append(ref[i, rows[0] : rows[1], :])
        ref, i = piece({0: g0, 1: g1, 3: g3}, (g2a, g2b), dy, dx)
        right.append(ref[i, :, at : at + SLOT])
    return jnp.concatenate(left, axis=1), jnp.concatenate(right, axis=0)


def multiply_near(g0, r0, g1, r1, g3, r3, out):
    refs = (r0, r1, r3, None, None, g0, g1, g3, None, None)
    pairs = [(dx, dy) for dx in (0, 1, 3) for dy in (0, 1, 3)]
    for n in range(BLOCK // SLOT):
        left, right = operands(refs, pairs, (0, BLOCK), n * SLOT)
        out[:, n * SLOT : (n + 1) * SLOT] = jnp.dot(left, right, preferred_element_type=f32)


def multiply_rest(odd, near, *refs):
    refs, outs = refs[:10], refs[10:]
    z0 = lax.axis_index("z0")
    half = BLOCK // 2
    rows = (odd * half, (odd + 1) * half)
    pairs = [(dx, dy) for dx in range(4) for dy in range(4) if dx == 2 or dy == 2]
    for n in range(BLOCK // SLOT):
        left, right = operands(refs, pairs, rows, n * SLOT)
        total = near[rows[0] : rows[1], n * SLOT : (n + 1) * SLOT]
        total = (total + jnp.dot(left, right, preferred_element_type=f32)).astype(bf16)
        for out, part in zip(outs, (total[: half // 2], total[half // 2 :])):
            if odd:
                out[(n - z0) & 3] = part[:128]
                out[4 + ((n + 1 - z0) & 3)] = part[128:]
            else:
                out[2 * n] = part[:128]
                out[2 * n + 1] = part[128:]


def add_odd(mine, other, up, down):
    for j in range(4):
        up[j] = (mine[j].astype(f32) + other[j].astype(f32)).astype(bf16)
        down[j] = (mine[4 + j].astype(f32) + other[4 + j].astype(f32)).astype(bf16)


def add_even(mine, other, up, down, *outs):
    for a, out in enumerate(outs):
        for h, ref in enumerate((up, down)):
            total = mine[2 * a + h].astype(f32) + other[2 * a + h].astype(f32) + ref[a].astype(f32)
            out[h * 128 : (h + 1) * 128, :] = total.astype(out.dtype)


def gram_part(t2, t1, t3, t0, head_grad, keep, send):
    total = (t0[...] + t1[...].astype(f32)) + (t2[...].astype(f32) + t3[...].astype(f32))
    part = total.astype(bf16)
    head_grad[...] = part
    gram = lax.dot_general(part, part, (((0,), (0,)), ((), ())), preferred_element_type=f32)
    first = jnp.concatenate([gram[:HEAD, :HEAD], gram[:HALF, HEAD:]], axis=0)
    second = jnp.concatenate([gram[HEAD:, HEAD:], gram[HALF:HEAD, HEAD:]], axis=0)
    core = lax.axis_index("core")
    keep[...] = jnp.where(core == 0, first, second)
    send[...] = jnp.where(core == 0, second, first)


def product(a, b):
    return jnp.dot(a, b, precision=lax.Precision.HIGHEST, preferred_element_type=f32)


def two_terms(a):
    top = a.astype(bf16)
    return top, (a - top.astype(f32)).astype(bf16)


def short_product(a, b):
    dot = functools.partial(jnp.dot, preferred_element_type=f32)
    return (dot(a[1], b[0]) + dot(a[0], b[1])) + dot(a[0], b[0])


def newton(meta, mine, other, head_grad, o0, o1, o2, o3, result):
    core = lax.axis_index("core")
    a, b = mine[...], other[...]
    first, second = jnp.where(core == 0, a, b), jnp.where(core == 0, b, a)
    corner = jnp.concatenate([first[HEAD:], second[HEAD:]], axis=0)
    gram = jnp.concatenate(
        [
            jnp.concatenate([first[:HEAD], corner], axis=1),
            jnp.concatenate([corner.T, second[:HEAD]], axis=1),
        ],
        axis=0,
    )
    zh = lax.axis_index("zh")
    pair = lax.axis_index("x") * 4 + zh < meta[PAIRS_AT]
    row = lax.broadcasted_iota(jnp.int32, (SLOT, SLOT), 0)
    col = lax.broadcasted_iota(jnp.int32, (SLOT, SLOT), 1)
    together = jnp.logical_or((row < HEAD) == (col < HEAD), pair)
    gram = jnp.where(together, gram, 0.0)
    on_diagonal = jnp.where(row == col, gram, 0.0)
    down = jnp.sum(on_diagonal, axis=0, keepdims=True)
    across = jnp.sum(on_diagonal, axis=1, keepdims=True)
    lane, line = col[:1, :], row[:, :1]

    def factor(squares, at, axis):
        low = jnp.sum(jnp.where(at < HEAD, squares, 0.0), axis=axis, keepdims=True)
        high = jnp.sum(jnp.where(at < HEAD, 0.0, squares), axis=axis, keepdims=True)
        norm = jnp.where(pair, low + high, jnp.where(at < HEAD, low, high))
        return 1.0 / (jnp.sqrt(norm) + epsilon)

    by_col = factor(down, lane, 1)
    by_row = factor(across, line, 0)
    gram = gram * by_row * by_col
    unit = jnp.where(row == col, 1.0, 0.0)
    factors = None
    for turn in range(NS_ITERS):
        multiplied = product if turn < 2 else lambda p, q: short_product(two_terms(p), two_terms(q))
        step = quintic_a * unit + quintic_b * gram + quintic_c * multiplied(gram, gram)
        if turn < NS_ITERS - 1:
            gram = multiplied(multiplied(gram, step), step)
        factors = step if factors is None else product(factors, step)
    top, middle = two_terms(factors)
    bottom = (factors - top.astype(f32) - middle.astype(f32)).astype(bf16)
    h = head_grad[...]
    update = jnp.dot(h, bottom, preferred_element_type=f32) + jnp.dot(h, middle, preferred_element_type=f32)
    update = update + jnp.dot(h, top, preferred_element_type=f32)
    result[...] = (update * (by_col * 64.0)).astype(bf16)
    for k, out in enumerate((o0, o1, o2, o3)):
        at = pl.multiple_of((zh ^ k) * HALF, HALF)
        out[...] = result[pl.ds(at, HALF), :]


def place_heads(other, meta, *refs):
    blocks, (out, rows, sem) = refs[:4], refs[-3:]
    ylo, x, zh = lax.axis_index("ylo"), lax.axis_index("x"), lax.axis_index("zh")
    for dx in range(4):
        for dzh in range(4):
            slot = (x ^ dx) * 4 + (zh ^ dzh)
            for j in range(2):
                at = pl.multiple_of(meta[PERM_AT + slot * 2 + j] * HEAD, HEAD)
                rows[:, pl.ds(at, HEAD)] = blocks[dx][dzh, :, j * HEAD : (j + 1) * HEAD].astype(f32)
    half = pl.ds(pl.multiple_of((ylo ^ other) * HALF, HALF), HALF)
    copy = pltpu.make_async_copy(rows, out.at[half, :], sem)
    copy.start()
    copy.wait()


Y_INDEX = (0, 2, 1, 3)


def move_x(a, k):
    return lax.ppermute(a, "x", [(i, i ^ (k & 3)) for i in range(4)])


def move_y(a, k):
    return lax.ppermute(a, ("ylo", "yhi"), [(Y_INDEX[i], Y_INDEX[i ^ (k & 3)]) for i in range(4)])


def move_z(a, k):
    return lax.ppermute(a, ("zh", "z0"), [(i, (i + k) % 8) for i in range(8)])


def swap(a, axis):
    return lax.ppermute(a, axis, [(0, 1), (1, 0)])


def farthest_first(arrays, move):
    opposite = move(arrays[2], 2)
    return [arrays[0], move(arrays[1], 1), opposite, move(arrays[3], 3)]


def far_to_front(arrays):
    return [arrays[2], arrays[0], arrays[1], arrays[3]]


def on_device(activations, cotangent, masked, ratios, owners):
    tok, width = activations.shape
    *blocks, meta = local_kernel(
        prepare,
        [shape((BLOCK, tok), bf16)] * 4 + [shape((tok, BLOCK), bf16)] * 4 + [shape((PERM_AT + HEADS,), jnp.int32)],
        (owners, ratios, masked[None, :], activations, cotangent),
        52,
        2 * tok * width,
        "prepare",
        in_specs=[hbm(), hbm(), vmem(), hbm(), hbm()],
        out_specs=[vmem()] * 8 + [smem()],
        scratch=[
            pltpu.VMEM((tok, width), bf16),
            pltpu.VMEM((tok, width), bf16),
            pltpu.SMEM((HEADS,), jnp.int32),
            pltpu.SMEM((1,), jnp.int32),
            pltpu.SMEM((HEADS,), jnp.int32),
            pltpu.SMEM((HEADS,), jnp.int32),
            pltpu.SemaphoreType.DMA((4,)),
        ],
    )
    rows, cols = blocks[:4], blocks[4:]
    r0, g0 = farthest_first(rows, move_y), farthest_first(cols, move_x)
    r0, g0 = jnp.stack(far_to_front(r0)), jnp.stack(far_to_front(g0))
    r1, r3 = move_x(r0, 1), move_x(r0, -1)
    g1, g3 = move_y(g0, 1), move_y(g0, -1)
    r2a, r2b = move_x(r1[:2], 3), move_x(r3[2:], 1)
    g2a, g2b = move_y(g1[:2], 3), move_y(g3[2:], 1)
    gathered = (r0, r1, r3, r2a, r2b, g0, g1, g3, g2a, g2b)

    flops = 2 * BLOCK * BLOCK * tok
    (near,) = local_kernel(
        multiply_near, [shape((BLOCK, BLOCK), f32)], (g0, r0, g1, r1, g3, r3), 32, 9 * flops, "multiply_near"
    )

    def rest(odd, name):
        return local_kernel(
            functools.partial(multiply_rest, odd),
            [shape((8, 128, SLOT), bf16)] * 2,
            (near, *gathered),
            32,
            7 * flops // 2,
            name,
        )

    own_odd, odd = rest(1, "multiply_odd")
    odd = swap(odd, "core")
    own_even, even = rest(0, "multiply_even")
    even = swap(even, "core")
    half_chunks = shape((4, 128, SLOT), bf16)
    up, down = local_kernel(
        add_odd, [half_chunks] * 2, (own_odd, odd), 8, 8 * 128 * SLOT, "add_odd"
    )
    up, down = move_z(up, 1), move_z(down, -1)
    t0, t1, t2, t3 = local_kernel(
        add_even,
        [shape((256, SLOT), f32)] + [shape((256, SLOT), bf16)] * 3,
        (own_even, even, up, down),
        8,
        16 * 128 * SLOT,
        "add_even",
    )
    t2 = move_z(t2, 4)
    t1, t3 = move_z(t1, 2), move_z(t3, 6)
    head_grad, mine, theirs = local_kernel(
        gram_part,
        [shape((256, SLOT), bf16), shape((GRAM, HEAD), f32), shape((GRAM, HEAD), f32)],
        (t2, t1, t3, t0),
        8,
        2 * 256 * SLOT * SLOT,
        "gram_part",
    )
    mine = mine + swap(theirs, "core")
    mine = mine + swap(mine, "z0")
    mine = (mine + move_y(mine, 2)) + (move_y(mine, 1) + move_y(mine, 3))
    update = local_kernel(
        newton,
        [shape((HALF, SLOT), bf16)] * 4,
        (meta, mine, swap(mine, "core"), head_grad),
        16,
        20 * 2 * SLOT**3 * 6,
        "newton",
        in_specs=[smem()] + [vmem()] * 3,
        scratch=[pltpu.VMEM((256, SLOT), bf16)],
    )
    ring = lambda a, k: lax.ppermute(a, "zh", [(i, i ^ (k & 3)) for i in range(4)])
    p0 = jnp.stack(farthest_first(update, ring))
    q0 = swap(p0, "ylo")
    ps = farthest_first([p0] * 4, move_x)
    qs = [q0, swap(ps[1], "ylo"), swap(ps[2], "ylo"), swap(ps[3], "ylo")]
    out = None
    for other, blocks in enumerate((ps, qs)):
        earlier = [] if out is None else [out]
        (out,) = local_kernel(
            functools.partial(place_heads, other),
            [shape((2 * HALF, width), f32)],
            (meta, *blocks, *earlier),
            12,
            0,
            "place_other" if other else "place_own",
            in_specs=[smem()] + [vmem()] * 4 + [hbm()] * len(earlier),
            out_specs=[hbm()],
            scratch=[pltpu.VMEM((HALF, width), f32), pltpu.SemaphoreType.DMA],
            aliases={5: 0} if earlier else {},
        )
    return out


def solution(mesh):
    axes = ("x", "ylo", "yhi", "zh", "z0", "core")
    fine = Mesh(mesh.devices.reshape(4, 2, 2, 4, 2, 2), axes)
    everywhere = P(axes)
    placed = (P(axes, None), P(axes, None), everywhere, everywhere, P())
    return jax.shard_map(
        on_device,
        mesh=fine,
        in_specs=placed,
        out_specs=P(("yhi", "zh", "z0", "core"), None),
        check_vma=False,
    )
```
